256 devices in a mesh: row: 4 (over y), col: 8 (over z), layer: 8 (over x, core).
Axes of the slice: x: 4, y: 4, z: 8, core: 2. Of those that a mesh axis runs over, the one named last changes fastest.
Arguments:
- left_blocks: bfloat16 [32, 512, 128, 128], P(('row', 'col'), 'layer'), may hold values from -6 to 6
- left_slots: int32 [32, 512], P(('row', 'col'), 'layer'), may hold values from 0 to 255, as said below
- right_blocks: bfloat16 [8, 128, 128, 128], P('layer', ('row', 'col')), may hold values from -6 to 6
- right_slots: int32 [8, 128], P('layer', ('row', 'col')), may hold values from 0 to 255, as said below
- out_slots: int32 [32, 32], P(('row', 'col')), may hold values from 0 to 63, as said below
Outputs:
- inflated: float32 [32, 32, 128, 128], P(('row', 'col'), 'layer')
The draws below stay inside these ranges and needn't reach their ends.
Inputs may be any that keep to these rules, and one draw needn't show every extreme that they name: `left_slots`: the 64 slots of one device differ from one another. `right_slots`: the slots of one layer differ from one another. `out_slots`: entry o of a row is r * 8 + o % 8; in each block column of the slab a row names 4 different block rows r.
All inputs are finite; a program needn't handle non-finite values.
Results may differ from the reference program's by a relative error of at most 0.0003.
Values may be sent and summed in bfloat16 or wider, within the bound.
A program may use at most 256 MiB of HBM per device.

```python
import jax
import jax.numpy as jnp
from jax import lax

BS = 128
RB_DEV = 8
KL = 32
SLAB_COLUMNS = 8
LNZ = 64
RNZ = 4
OUT_DEV = 32
N_ROW = 4
N_COL = 8
N_LAYER = 8


def draw_left_slots(key, part):
    key = jax.random.fold_in(key, 11)
    many_keys = jax.random.split(key, N_ROW * N_COL * N_LAYER)
    chosen = jax.vmap(lambda one_key: jax.random.permutation(one_key, RB_DEV * KL)[:LNZ])(many_keys)
    return chosen.reshape(N_ROW * N_COL, N_LAYER * LNZ).astype(jnp.int32)


def draw_right_slots(key, part):
    key = jax.random.fold_in(key, 23)
    many_keys = jax.random.split(key, N_LAYER)
    chosen = jax.vmap(lambda one_key: jax.random.permutation(one_key, KL * SLAB_COLUMNS)[:N_ROW * N_COL * RNZ])(many_keys)
    return chosen.astype(jnp.int32)


def draw_out_slots(key, part):
    key = jax.random.fold_in(key, 37)
    many_keys = jax.random.split(key, N_ROW * N_COL * SLAB_COLUMNS)
    many_keys = many_keys.reshape((N_ROW * N_COL, SLAB_COLUMNS) + many_keys.shape[1:])
    half_rows = RB_DEV // 2

    def one_column(one_key):
        return jax.random.permutation(one_key, RB_DEV)[:half_rows]
    picked = jax.vmap(jax.vmap(one_column))(many_keys)
    columns = jnp.arange(SLAB_COLUMNS, dtype=jnp.int32)[None, :, None]
    slots = picked.astype(jnp.int32) * SLAB_COLUMNS + columns
    slots = jnp.transpose(slots, (0, 2, 1))
    return slots.reshape(N_ROW * N_COL, OUT_DEV).astype(jnp.int32)


def levels(key, dims, pieces, smallest, top_value):
    gain = 1.0
    for position, shards_of in pieces:
        heights = jax.random.uniform(jax.random.fold_in(jax.random.fold_in(key, 6), position), (shards_of,), jnp.float32, smallest / len(pieces), top_value / len(pieces))
        gain = gain * jnp.repeat(jnp.exp(heights), dims[position] // shards_of).reshape((-1,) + (1,) * (len(dims) - 1 - position))
    return gain


def gaussian(own_key, dims, width, limit, shards=(), kind=jnp.bfloat16):
    entries = jax.random.normal(own_key, dims, jnp.float32) * width
    if len(shards) > 0:
        entries = levels(own_key, dims, shards, -0.22, 0.18) * entries
    return jnp.clip(entries, min=-limit, max=limit).astype(kind)


def setup_inputs(seed: int = 0) -> dict:
    arg_keys = jax.random.split(jax.random.key(seed), 6)
    return {
        "left_blocks": gaussian(arg_keys[0], (N_ROW * N_COL, N_LAYER * LNZ, BS, BS), 1.0, 6.0, ((0, 32), (1, 8))),
        "left_slots": draw_left_slots(jax.random.fold_in(arg_keys[5], 71), 0),
        "right_blocks": gaussian(arg_keys[2], (N_LAYER, N_ROW * N_COL * RNZ, BS, BS), 1.0, 6.0, ((0, 8), (1, 32))),
        "right_slots": draw_right_slots(jax.random.fold_in(arg_keys[5], 71), 0),
        "out_slots": draw_out_slots(jax.random.fold_in(arg_keys[5], 71), 0),
    }


def dense_grid(block_set, block_slots, major_count, minor_count):
    block_side = block_set.shape[-1]
    block_grid = jnp.zeros((major_count * minor_count, block_side, block_side), block_set.dtype)
    block_grid = block_grid.at[block_slots].set(block_set)
    block_grid = block_grid.reshape(major_count, minor_count, block_side, block_side).transpose(0, 2, 1, 3)
    return block_grid.reshape(major_count * block_side, minor_count * block_side)


def select_blocks(product, sparsity_pattern, row_count, number_of_slabs):
    block_side = product.shape[0] // row_count
    block_grid = product.reshape(row_count, block_side, number_of_slabs, block_side)
    return block_grid[sparsity_pattern // number_of_slabs, :, sparsity_pattern % number_of_slabs, :]


def column_totals(expanded_matrix, sparsity_pattern, number_of_slabs):
    row_sums = jnp.sum(expanded_matrix, axis=1)
    onehot = (sparsity_pattern[:, None] % number_of_slabs == jnp.arange(number_of_slabs)[None, :]).astype(jnp.float32)
    return jnp.einsum('ns,nc->sc', onehot, row_sums, precision=lax.Precision.HIGHEST)


def apply_inflation(expanded_matrix, sparsity_pattern, number_of_slabs, column_mean):
    onehot = (sparsity_pattern[:, None] % number_of_slabs == jnp.arange(number_of_slabs)[None, :]).astype(jnp.float32)
    spread = jnp.einsum('ns,sc->nc', onehot, column_mean, precision=lax.Precision.HIGHEST)
    return expanded_matrix / (spread[:, None, :] + 1e-6)


def reference(left_blocks, left_slots, right_blocks, right_slots, out_slots):
    cells = N_ROW * N_COL
    block_side = left_blocks.shape[-1]
    right_dense = jnp.stack([dense_grid(right_blocks[layer_pos].astype(jnp.float32), right_slots[layer_pos], KL, SLAB_COLUMNS) for layer_pos in range(N_LAYER)])
    right_dense = right_dense.reshape(N_LAYER, KL, block_side, SLAB_COLUMNS * block_side)
    left_split = left_blocks.reshape(cells, N_LAYER, LNZ, block_side, block_side)
    slot_split = left_slots.reshape(cells, N_LAYER, LNZ)

    def cell_product(cell_args):
        cell_blocks, cell_slots, cell_pattern = cell_args

        def layer_step(running, layer_args):
            layer_blocks, layer_slots, layer_right = layer_args
            right_strips = layer_right[layer_slots % KL]
            contrib = jnp.einsum('nab,nbc->nac', layer_blocks.astype(jnp.float32), right_strips, precision=lax.Precision.HIGHEST)
            layer_part = jax.ops.segment_sum(contrib, (layer_slots // KL).astype(jnp.int32), num_segments=RB_DEV)
            return running + layer_part, None

        zero_sum = jnp.zeros((RB_DEV, block_side, SLAB_COLUMNS * block_side), jnp.float32)
        summed, unused = lax.scan(layer_step, zero_sum, (cell_blocks, cell_slots, right_dense))
        product = summed.reshape(RB_DEV * block_side, SLAB_COLUMNS * block_side)
        chosen = select_blocks(product, cell_pattern, RB_DEV, SLAB_COLUMNS)
        return chosen * chosen

    expanded_matrix = lax.map(cell_product, (left_split, slot_split, out_slots))
    flattened_squared = expanded_matrix.reshape(cells * OUT_DEV, block_side, block_side)
    flattened_pattern = out_slots.reshape(cells * OUT_DEV)
    overall_rows = cells * (RB_DEV // 2) * block_side
    column_mean = column_totals(flattened_squared, flattened_pattern, SLAB_COLUMNS) / overall_rows
    inflated = apply_inflation(flattened_squared, flattened_pattern, SLAB_COLUMNS, column_mean)
    return inflated.reshape(cells, OUT_DEV, block_side, block_side)
```

```python
import jax
import jax.numpy as jnp
from jax import lax
from jax.experimental import pallas as pl
from jax.experimental.pallas import tpu as pltpu
from jax.sharding import PartitionSpec as P

MESH = pl.DeviceIdType.MESH
F32 = jnp.float32
BF16 = jnp.bfloat16
I32 = jnp.int32

BS = 128
NY, NZ, NX = 4, 8, 4
ROWS = 4 * BS
A_ROWS, B_ROWS = 304, 208
A_CUT, B_CUT = 160, 96
Z_INDEX = {0: 0, 1: 1, -1: 2, 2: 3, -2: 4, 3: 5, -3: 6, 4: 7}
Y_INDEX = {0: 0, 1: 1, -1: 2, 2: 3}
SOURCES = (
    (0, 0), (0, 1), (0, 2), (1, 0), (2, 0), (1, 1), (1, 2), (2, 1), (2, 2), (3, 0), (0, 3), (0, 4),
    (3, 1), (3, 2), (1, 3), (2, 3), (1, 4), (2, 4), (0, 6), (1, 5), (2, 5), (1, 6), (2, 6), (3, 3),
    (3, 4), (0, 5), (3, 5), (3, 6), (1, 7), (2, 7), (3, 7), (0, 7),
)
GROUPS = (4, 6, 8, 2, 4, 4, 4)
PROGRAM = (
    0, 200, 4, 6, 14, 10, 12, 32, 36, -5, 5, -1, -7, -15, 1, 7, 16, 18, -11, -13, -33, -37, 201,
    202, 203, 204, 11, 13, 40, 44, 15, 37, 400, -6, 300, -2, -8, 2, 8, 20, 22, 33, 300, -17, -19,
    17, 19, -41, -45, 205, 206, 207, 208, -12, 48, 52, 45, -14, -16, 209, 300, -38, 210, -3, 3, 41,
    300, 300, -34, 211, -9, 9, 24, 26, -21, 21, -49, -53, 49, 53, 34, -23, -4, -18, -20, 212, 213,
    -46, 214, 215, 46, -10, 28, 30, 23, -42, 216, 217, 42, 300, -54, 54, 38, -50, 50, 300, -25, 25,
    -27, 27, -35, 218, 35, 300, 300, -22, -47, 219, 220, 47, -31, 31, 300, -55, 55, -43, 221, 222,
    43, -29, 29, -24, 223, 224, 300, -39, 225, 39, -51, 51, -36, 300, -26, -28, 226, 227, -48, -44,
    228, 229, -56, -32, -30, 300, -52, 230, -40, 231, 300, 300, 300,
)
STEP = 8
NG = len(GROUPS)
NONE = 128


def wrap(value, count):
    value = value % count
    return value - count if value > count // 2 else value


def gather_copies():
    copies = []

    def part(kind, sign, whole):
        size, cut = (A_ROWS, A_CUT) if kind == 0 else (B_ROWS, B_CUT)
        if whole:
            return 0, size
        return (0, cut) if sign == 1 else (cut, size - cut)

    for sign in (1, -1):
        for d in range(1, 5):
            src = ((0, 1), (Z_INDEX[-sign * (d - 1)], 1))
            dst = ((0, 1), (Z_INDEX[wrap(-sign * d, NZ)], 1))
            copies.append((0, 1, sign, src, dst) + part(0, sign, d < 4) + (d == 1,))
        for d in (1, 2):
            src = ((0, 1), (Y_INDEX[-sign * (d - 1)], 1))
            dst = ((0, 1), (Y_INDEX[wrap(-sign * d, NY)], 1))
            copies.append((1, 0, sign, src, dst) + part(1, sign, d < 2) + (d == 1,))
    for first, count in ((0, 1), (1, 2), (3, 2), (5, 2), (7, 1)):
        for sign in (1, -1):
            for d in (1, 2):
                src = ((Y_INDEX[-sign * (d - 1)], 1), (first, count))
                dst = ((Y_INDEX[wrap(-sign * d, NY)], 1), (first, count))
                own = first == 0 and d == 1
                copies.append((0, 0, sign, src, dst) + part(0, sign, d < 2) + (own,))
    for first, count in ((0, 1), (1, 2), (3, 1)):
        for sign in (1, -1):
            for d in range(1, 5):
                src = ((Z_INDEX[-sign * (d - 1)], 1), (first, count))
                dst = ((Z_INDEX[wrap(-sign * d, NZ)], 1), (first, count))
                own = first == 0 and d == 1
                copies.append((1, 1, sign, src, dst) + part(1, sign, d < 4) + (own,))
    return copies


COPIES = gather_copies()
N_SMALL = 7 + 3
N_X = 4 * 6
N_SUM = 15 + 7
SEND_SMALL = len(COPIES)
SEND_SIB = SEND_SMALL + N_SMALL
SEND_X = SEND_SIB + 4
SEND_SUM = SEND_X + N_X
N_SEM = SEND_SUM + N_SUM


def to_column(row, eye):
    return jnp.sum(jnp.where(eye, jnp.broadcast_to(row, (BS, BS)), 0), axis=1, keepdims=True)


def kernel(
    left_slots, right_slots, out_slots, left, right, squares, sums,
    left_set, gather_a, gather_b, stage, products, slots_row, slots, meta, meta_s,
    left_s, right_s, out_s, sib_send, sib_recv, partial, half_recv, full_recv,
    sums_xy, sums_z, squared, send_sem, recv_sem, local_sem,
):
    y, z, layer = lax.axis_index("row"), lax.axis_index("col"), lax.axis_index("layer")
    x, core = layer // 2, lax.rem(layer, 2)

    def along_y(d):
        return (lax.rem(y + (d % NY), NY), z, layer)

    def along_z(d):
        return (y, lax.rem(z + (d % NZ), NZ), layer)

    def along_xy(dx, dy):
        return (lax.rem(y + dy % NY, NY), z, lax.rem(x + dx % NX, NX) * 2 + core)

    sibling = (y, z, x * 2 + (1 - core))
    xy_peers = [(dx, dy) for dx in range(NX) for dy in range(NY) if dx or dy]

    local = [
        pltpu.make_async_copy(right_slots, right_s, local_sem.at[0]),
        pltpu.make_async_copy(left_slots, left_s, local_sem.at[1]),
        pltpu.make_async_copy(out_slots, out_s, local_sem.at[2]),
        pltpu.make_async_copy(left, left_set.at[pl.ds(0, 64)], local_sem.at[3]),
    ] + [
        pltpu.make_async_copy(right.at[pl.ds(q * BS, BS)], stage.at[q], local_sem.at[4 + q])
        for q in range(4)
    ]
    for copy in local:
        copy.start()

    barrier = pltpu.get_barrier_semaphore()
    peers = [along_z(d) for d in range(1, NZ)] + [along_xy(*p) for p in xy_peers] + [sibling]
    for peer in peers:
        pl.semaphore_signal(barrier, 1, device_id=peer, device_id_type=MESH)
    pl.semaphore_wait(barrier, len(peers))

    def remote(number, src, dst, device):
        return pltpu.make_async_remote_copy(
            src_ref=src, dst_ref=dst, send_sem=send_sem.at[number], recv_sem=recv_sem.at[number],
            device_id=device, device_id_type=MESH,
        )

    def gather_copy(n):
        kind, axis, sign, src, dst, row, rows, own = COPIES[n]
        buffer = gather_a if kind == 0 else gather_b

        def place(where):
            (p, _), (q, qn) = where
            if qn == 1:
                return buffer.at[p, q, pl.ds(row, rows)]
            return buffer.at[p, pl.ds(q, qn), pl.ds(row, rows)]

        source = right.at[pl.ds((0 if kind == 0 else A_ROWS) + row, rows)] if own else place(src)
        return remote(n, source, place(dst), along_z(sign) if axis else along_y(sign))

    def small_copy(n):
        if n < 7:
            d = n + 1
            return remote(
                SEND_SMALL + n, slots.at[0, 0], slots.at[0, Z_INDEX[wrap(-d, NZ)]], along_z(d)
            )
        d = n - 6
        return remote(SEND_SMALL + n, slots.at[0], slots.at[Y_INDEX[wrap(-d, NY)]], along_y(d))

    lane = lax.broadcasted_iota(I32, (1, BS), 1)

    def send_slots():
        local[0].wait()
        row = jnp.zeros((1, BS), I32)
        for q in range(4):
            row = jnp.where((lane & 3) == q, right_s[0, q], row)
        slots[0, 0] = row
        for n in range(7):
            small_copy(n).start()

    def forward_slots():
        for n in range(7):
            small_copy(n).wait_recv()
        for n in range(7, N_SMALL):
            small_copy(n).start()

    def sort_slots():
        for n in range(7, N_SMALL):
            small_copy(n).wait_recv()
        row_id = lax.broadcasted_iota(I32, (BS, BS), 0)
        lane_id = lax.broadcasted_iota(I32, (BS, BS), 1)
        eye = row_id == lane_id
        slot = jnp.zeros((1, BS), I32)
        for p, (yi, zi) in enumerate(SOURCES):
            slot = jnp.where((lane >> 2) == p, slots[yi, zi], slot)
        group = jnp.zeros((1, BS), I32)
        first = 0
        for size in GROUPS[:-1]:
            first += size
            group = group + ((lane >> 2) >= first).astype(I32)
        segment = group * 8 + (slot & 7)
        key = segment * BS + lane
        key_column = to_column(key, eye)
        rank = jnp.sum((key_column < key).astype(I32), axis=0, keepdims=True)
        segment_column = key_column >> 7
        before = jnp.sum((segment_column < segment).astype(I32), axis=0, keepdims=True)
        opens = (before == rank).astype(I32)
        packed = (rank << 16) | (opens << 15) | (slot << 7) | lane
        packed_column = to_column(packed, eye)
        here = (packed_column >> 16) == lane_id
        meta[0:1, :] = jnp.sum(jnp.where(here, packed_column & 0xFFFF, 0), axis=0, keepdims=True)
        upto = jnp.sum((segment_column <= lane_id).astype(I32), axis=0, keepdims=True)
        count = jnp.sum((segment_column == lane_id).astype(I32), axis=0, keepdims=True)
        meta[1:2, :] = jnp.where(count > 0, upto - 1, NONE)
        local[1].wait()
        inverse = [jnp.full((1, BS), 64, I32), jnp.full((1, BS), 64, I32)]
        for n in range(64):
            place = left_s[0, n]
            for h in range(2):
                inverse[h] = jnp.where(lane + h * BS == place, n, inverse[h])
        meta[2:3, :] = inverse[0]
        meta[3:4, :] = inverse[1]
        copy = pltpu.make_async_copy(meta, meta_s, local_sem.at[8])
        copy.start()
        copy.wait()
        for copy in local[2:]:
            copy.wait()

    def stage_source(p):
        if p == 0:
            return
        yi, zi = SOURCES[p]
        a_tail = A_ROWS - 2 * BS
        b_head = BS - a_tail
        stage[4 * p] = gather_a[yi, zi, pl.ds(0, BS)]
        stage[4 * p + 1] = gather_a[yi, zi, pl.ds(BS, BS)]
        stage[4 * p + 2, pl.ds(0, a_tail)] = gather_a[yi, zi, pl.ds(2 * BS, a_tail)]
        stage[4 * p + 2, pl.ds(a_tail, b_head)] = gather_b[zi, yi, pl.ds(0, b_head)]
        stage[4 * p + 3] = gather_b[zi, yi, pl.ds(b_head, BS)]

    def multiply(start):
        for t in range(start, start + STEP):
            word = meta_s[0, t]
            block, slot, opens = word & 127, (word >> 7) & 255, word >> 15
            k, j = slot >> 3, slot & 7
            chosen = []
            for m in range(4):
                r = out_s[0, lax.rem(x + m, NX) * 8 + j] >> 3
                at = r * 32 + k
                chosen.append(left_set[meta_s[2 + (at >> 7), at & 127]])
            product = jnp.dot(
                jnp.concatenate(chosen, axis=0), stage[block], preferred_element_type=F32
            )
            previous = opens * NONE + (1 - opens) * (t - 1)
            products[t] = product + products[previous]

    left_set[64] = jnp.zeros((BS, BS), BF16)
    products[NONE] = jnp.zeros((ROWS, BS), F32)

    done = 0
    opened = 0
    for item in PROGRAM:
        if item < 0:
            gather_copy(-1 - item).wait_recv()
        elif item < 200:
            gather_copy(item).start()
            opened += 1
            if opened == 8:
                send_slots()
        elif item < 300:
            if item == 201:
                forward_slots()
            stage_source(item - 200)
        elif item == 300:
            multiply(done)
            done += STEP
        else:
            sort_slots()

    def column_sum(j):
        total = products[meta_s[1, j]]
        for g in range(1, NG):
            total = total + products[meta_s[1, g * 8 + j]]
        return total

    def sib_copy(jj):
        return remote(SEND_SIB + jj, sib_send.at[jj], sib_recv.at[jj], sibling)

    for jj in range(4):
        sib_send[jj] = column_sum((1 - core) * 4 + jj)
        sib_copy(jj).start()
    for jj in range(4):
        partial[jj] = column_sum(core * 4 + jj)

    half = BS // 2

    def x_copy(jj, what):
        number = SEND_X + jj * 6 + what
        forth = what % 2 == 0
        side = 0 if forth else 1
        device = along_xy(1, 0) if forth else along_xy(-1, 0)
        if what < 2:
            src = partial.at[jj, pl.ds(2 * BS + side * half, half)]
            dst = half_recv.at[side, jj]
        else:
            base = BS if forth else 3 * BS
            row = (half if forth else 0) if what < 4 else (0 if forth else half)
            src = partial.at[jj, pl.ds(base + row, half)]
            dst = full_recv.at[side, jj, pl.ds(row, half)]
        return remote(number, src, dst, device)

    for jj in range(4):
        sib_copy(jj).wait_recv()
        partial[jj] = partial[jj] + sib_recv[jj]
        x_copy(jj, 0).start()
        x_copy(jj, 1).start()
    for jj in range(4):
        x_copy(jj, 2).start()
        x_copy(jj, 3).start()
    for jj in range(4):
        x_copy(jj, 0).wait_recv()
        partial[jj, pl.ds(BS, half)] = partial[jj, pl.ds(BS, half)] + half_recv[0, jj]
        x_copy(jj, 4).start()
        x_copy(jj, 1).wait_recv()
        partial[jj, pl.ds(3 * BS + half, half)] = (
            partial[jj, pl.ds(3 * BS + half, half)] + half_recv[1, jj]
        )
        x_copy(jj, 5).start()
    stores = []
    for jj in range(4):
        for what in (2, 3, 4, 5):
            x_copy(jj, what).wait_recv()
        total = partial[jj, pl.ds(0, BS)] + full_recv[0, jj] + full_recv[1, jj]
        square = total * total
        squared[jj] = square
        stores.append(pltpu.make_async_copy(squared.at[jj], squares.at[jj], local_sem.at[9 + jj]))
        stores[-1].start()
        sums_xy[0, jj : jj + 1, :] = jnp.sum(square, axis=0, keepdims=True)

    def xy_copy(n):
        dx, dy = xy_peers[n]
        slot = ((-dx) % NX) * NY + (-dy) % NY
        return remote(SEND_SUM + n, sums_xy.at[0], sums_xy.at[slot], along_xy(dx, dy))

    def z_copy(n):
        d = n + 1
        return remote(SEND_SUM + 15 + n, sums_z.at[0], sums_z.at[(-d) % NZ], along_z(d))

    for n in range(15):
        xy_copy(n).start()
    total = sums_xy[0]
    for n in range(15):
        xy_copy(n).wait_recv()
    for n in range(1, 16):
        total = total + sums_xy[n]
    sums_z[0] = total
    for n in range(7):
        z_copy(n).start()
    for n in range(7):
        z_copy(n).wait_recv()
    for n in range(1, NZ):
        total = total + sums_z[n]
    meta_sum = sums_xy.at[1]
    meta_sum[...] = total
    last = pltpu.make_async_copy(meta_sum, sums, local_sem.at[13])
    last.start()

    for n in range(len(COPIES)):
        gather_copy(n).wait_send()
    for n in range(N_SMALL):
        small_copy(n).wait_send()
    for jj in range(4):
        sib_copy(jj).wait_send()
        for what in range(6):
            x_copy(jj, what).wait_send()
        stores[jj].wait()
    for n in range(15):
        xy_copy(n).wait_send()
    for n in range(7):
        z_copy(n).wait_send()
    last.wait()


def body(left_blocks, left_slots, right_blocks, right_slots, out_slots):
    any_spec = pl.BlockSpec(memory_space=pl.ANY)
    squares, sums = pl.pallas_call(
        kernel,
        out_shape=(
            jax.ShapeDtypeStruct((4, BS, BS), F32),
            jax.ShapeDtypeStruct((4, BS), F32),
        ),
        in_specs=[any_spec] * 5,
        out_specs=(any_spec, any_spec),
        scratch_shapes=[
            pltpu.VMEM((65, BS, BS), BF16),
            pltpu.VMEM((NY, NZ, A_ROWS, BS), BF16),
            pltpu.VMEM((NZ, NY, B_ROWS, BS), BF16),
            pltpu.VMEM((32 * 4, BS, BS), BF16),
            pltpu.VMEM((NONE + 1, ROWS, BS), F32),
            pltpu.VMEM((1, BS), I32),
            pltpu.VMEM((NY, NZ, 1, BS), I32),
            pltpu.VMEM((8, BS), I32),
            pltpu.SMEM((8, BS), I32),
            pltpu.SMEM((1, 64), I32),
            pltpu.SMEM((1, 4), I32),
            pltpu.SMEM((1, 32), I32),
            pltpu.VMEM((4, ROWS, BS), F32),
            pltpu.VMEM((4, ROWS, BS), F32),
            pltpu.VMEM((4, ROWS, BS), F32),
            pltpu.VMEM((2, 4, BS // 2, BS), F32),
            pltpu.VMEM((2, 4, BS, BS), F32),
            pltpu.VMEM((16, 4, BS), F32),
            pltpu.VMEM((NZ, 4, BS), F32),
            pltpu.VMEM((4, BS, BS), F32),
            pltpu.SemaphoreType.DMA((N_SEM,)),
            pltpu.SemaphoreType.DMA((N_SEM,)),
            pltpu.SemaphoreType.DMA((14,)),
        ],
        compiler_params=pltpu.CompilerParams(
            collective_id=0, has_side_effects=True, vmem_limit_bytes=60 * 2**20
        ),
        name="expand_and_sum",
    )(
        left_slots,
        right_slots,
        out_slots,
        left_blocks.reshape(64, BS, BS),
        right_blocks.reshape(ROWS, BS),
    )
    rows = NY * NZ * 4 * BS
    return (squares / (sums[:, None, :] / rows + 1e-6))[None]


def solution(mesh):
    return jax.shard_map(
        body,
        mesh=mesh,
        in_specs=(
            P(("row", "col"), "layer", None, None),
            P(("row", "col"), "layer"),
            P("layer", ("row", "col"), None, None),
            P("layer", ("row", "col")),
            P(("row", "col"), None),
        ),
        out_specs=P(("row", "col"), "layer", None, None),
        check_vma=False,
    )
```

```python
import jax
import jax.numpy as jnp
from jax import lax
from jax.experimental import pallas as pl
from jax.experimental.pallas import tpu as pltpu
from jax.sharding import PartitionSpec as P

MESH = pl.DeviceIdType.MESH
F32 = jnp.float32
BF16 = jnp.bfloat16
I32 = jnp.int32

BS = 128
NY, NZ, NX = 4, 8, 4
ROWS = 4 * BS
A_ROWS, B_ROWS = 304, 208
A_CUT, B_CUT = 160, 96
Z_INDEX = {0: 0, 1: 1, -1: 2, 2: 3, -2: 4, 3: 5, -3: 6, 4: 7}
Y_INDEX = {0: 0, 1: 1, -1: 2, 2: 3}
SOURCES = (
    (0, 0), (0, 1), (0, 2), (1, 0), (2, 0), (0, 3), (1, 2), (2, 2), (1, 1), (2, 1), (0, 4), (0, 5),
    (3, 1), (3, 2), (3, 0), (1, 4), (2, 4), (1, 3), (2, 3), (3, 4), (3, 3), (0, 6), (1, 5), (2, 5),
    (1, 6), (2, 6), (0, 7), (3, 5), (3, 6), (1, 7), (2, 7), (3, 7),
)
GROUPS = (4, 6, 8, 4, 4, 2, 2, 2)
PROGRAM = (
    6, 4, 0, 10, 401, 36, 32, 14, 200, 12, -5, -11, 11, 5, -7, 7, -1, 1, 16, 18, -33, -13, 13, 40,
    -37, 201, 37, -15, 402, 202, -6, 33, -12, 44, -8, 8, -2, 20, 22, 2, -41, -19, -38, 203, 38, 48,
    -17, 52, 400, -34, 15, 204, -45, 205, 206, 19, 41, 45, 17, -14, 207, -3, 3, -9, -23, 34, 23,
    300, -16, -21, 21, 300, 208, -39, 24, 26, 209, 300, -49, 9, -53, 210, 49, -20, 211, -18, 53,
    300, 212, 300, 213, -42, 214, 215, 42, 216, -4, -24, -22, -46, 46, 217, 39, 300, 218, -10, 28,
    30, 300, 300, -50, 219, 50, 300, -54, 54, -35, -27, 35, 27, 220, 221, 300, -25, 25, 300, -47,
    -43, 222, 223, 224, -31, 47, 43, 31, 225, 300, -40, -29, -51, 300, -55, 29, -28, -36, 51, 55,
    500, 226, -26, 227, 228, 300, -48, -44, -32, 229, 300, -52, -56, 230, -30, 231, 300,
)
STEP = 8
NG = len(GROUPS)
FOLDED = 5
NONE = 128


def wrap(value, count):
    value = value % count
    return value - count if value > count // 2 else value


def gather_copies():
    copies = []

    def part(kind, sign, whole):
        size, cut = (A_ROWS, A_CUT) if kind == 0 else (B_ROWS, B_CUT)
        if whole:
            return 0, size
        return (0, cut) if sign == 1 else (cut, size - cut)

    for sign in (1, -1):
        for d in range(1, 5):
            src = ((0, 1), (Z_INDEX[-sign * (d - 1)], 1))
            dst = ((0, 1), (Z_INDEX[wrap(-sign * d, NZ)], 1))
            copies.append((0, 1, sign, src, dst) + part(0, sign, d < 4) + (d == 1,))
        for d in (1, 2):
            src = ((0, 1), (Y_INDEX[-sign * (d - 1)], 1))
            dst = ((0, 1), (Y_INDEX[wrap(-sign * d, NY)], 1))
            copies.append((1, 0, sign, src, dst) + part(1, sign, d < 2) + (d == 1,))
    for first, count in ((0, 1), (1, 2), (3, 2), (5, 2), (7, 1)):
        for sign in (1, -1):
            for d in (1, 2):
                src = ((Y_INDEX[-sign * (d - 1)], 1), (first, count))
                dst = ((Y_INDEX[wrap(-sign * d, NY)], 1), (first, count))
                own = first == 0 and d == 1
                copies.append((0, 0, sign, src, dst) + part(0, sign, d < 2) + (own,))
    for first, count in ((0, 1), (1, 2), (3, 1)):
        for sign in (1, -1):
            for d in range(1, 5):
                src = ((Z_INDEX[-sign * (d - 1)], 1), (first, count))
                dst = ((Z_INDEX[wrap(-sign * d, NZ)], 1), (first, count))
                own = first == 0 and d == 1
                copies.append((1, 1, sign, src, dst) + part(1, sign, d < 4) + (own,))
    return copies


COPIES = gather_copies()
N_SMALL = 7 + 3
N_X = 4 * 6
N_SUM = 15 + 7
SEND_SMALL = len(COPIES)
SEND_SIB = SEND_SMALL + N_SMALL
SEND_X = SEND_SIB + 4
SEND_SUM = SEND_X + N_X
N_SEM = SEND_SUM + N_SUM


def to_column(row, eye):
    return jnp.sum(jnp.where(eye, jnp.broadcast_to(row, (BS, BS)), 0), axis=1, keepdims=True)


def kernel(
    left_slots, right_slots, out_slots, left, right, squares, sums,
    left_set, gather_a, gather_b, stage, products, slots_row, slots, meta, meta_s,
    left_s, right_s, out_s, sib_send, sib_recv, partial, half_recv, full_recv,
    sums_xy, sums_z, squared, send_sem, recv_sem, local_sem,
):
    y, z, layer = lax.axis_index("row"), lax.axis_index("col"), lax.axis_index("layer")
    x, core = layer // 2, lax.rem(layer, 2)

    def along_y(d):
        return (lax.rem(y + (d % NY), NY), z, layer)

    def along_z(d):
        return (y, lax.rem(z + (d % NZ), NZ), layer)

    def along_xy(dx, dy):
        return (lax.rem(y + dy % NY, NY), z, lax.rem(x + dx % NX, NX) * 2 + core)

    sibling = (y, z, x * 2 + (1 - core))
    xy_peers = [(dx, dy) for dx in range(NX) for dy in range(NY) if dx or dy]
    xy_peers.sort(key=lambda p: -min(p[0], NX - p[0]) - min(p[1], NY - p[1]))

    local = [
        pltpu.make_async_copy(right_slots, right_s, local_sem.at[0]),
        pltpu.make_async_copy(left_slots, left_s, local_sem.at[1]),
        pltpu.make_async_copy(out_slots, out_s, local_sem.at[2]),
        pltpu.make_async_copy(left, left_set.at[pl.ds(0, 64)], local_sem.at[3]),
    ] + [
        pltpu.make_async_copy(right.at[pl.ds(q * BS, BS)], stage.at[q], local_sem.at[4 + q])
        for q in range(4)
    ]
    for copy in local:
        copy.start()

    barrier = pltpu.get_barrier_semaphore()
    peers = [along_z(d) for d in range(1, NZ)] + [along_y(d) for d in range(1, NY)]
    peers += [along_xy(1, 0), along_xy(-1, 0), sibling]
    for peer in peers:
        pl.semaphore_signal(barrier, 1, device_id=peer, device_id_type=MESH)
    pl.semaphore_wait(barrier, len(peers))

    def remote(number, src, dst, device):
        return pltpu.make_async_remote_copy(
            src_ref=src, dst_ref=dst, send_sem=send_sem.at[number], recv_sem=recv_sem.at[number],
            device_id=device, device_id_type=MESH,
        )

    def gather_copy(n):
        kind, axis, sign, src, dst, row, rows, own = COPIES[n]
        buffer = gather_a if kind == 0 else gather_b

        def place(where):
            (p, _), (q, qn) = where
            if qn == 1:
                return buffer.at[p, q, pl.ds(row, rows)]
            return buffer.at[p, pl.ds(q, qn), pl.ds(row, rows)]

        source = right.at[pl.ds((0 if kind == 0 else A_ROWS) + row, rows)] if own else place(src)
        return remote(n, source, place(dst), along_z(sign) if axis else along_y(sign))

    def small_copy(n):
        if n < 7:
            d = n + 1
            return remote(
                SEND_SMALL + n, slots.at[0, 0], slots.at[0, Z_INDEX[wrap(-d, NZ)]], along_z(d)
            )
        d = n - 6
        return remote(SEND_SMALL + n, slots.at[0], slots.at[Y_INDEX[wrap(-d, NY)]], along_y(d))

    lane = lax.broadcasted_iota(I32, (1, BS), 1)

    def send_slots():
        local[0].wait()
        row = jnp.zeros((1, BS), I32)
        for q in range(4):
            row = jnp.where((lane & 3) == q, right_s[0, q], row)
        slots[0, 0] = row
        for n in range(7):
            small_copy(n).start()

    def forward_slots():
        for n in range(7):
            small_copy(n).wait_recv()
        for n in range(7, N_SMALL):
            small_copy(n).start()

    def sort_slots():
        for n in range(7, N_SMALL):
            small_copy(n).wait_recv()
        row_id = lax.broadcasted_iota(I32, (BS, BS), 0)
        lane_id = lax.broadcasted_iota(I32, (BS, BS), 1)
        eye = row_id == lane_id
        slot = jnp.zeros((1, BS), I32)
        for p, (yi, zi) in enumerate(SOURCES):
            slot = jnp.where((lane >> 2) == p, slots[yi, zi], slot)
        group = jnp.zeros((1, BS), I32)
        first = 0
        for size in GROUPS[:-1]:
            first += size
            group = group + ((lane >> 2) >= first).astype(I32)
        segment = group * 8 + (slot & 7)
        key = segment * BS + lane
        key_column = to_column(key, eye)
        rank = jnp.sum((key_column < key).astype(I32), axis=0, keepdims=True)
        segment_column = key_column >> 7
        before = jnp.sum((segment_column < segment).astype(I32), axis=0, keepdims=True)
        opens = (before == rank).astype(I32)
        packed = (rank << 16) | (opens << 15) | (slot << 7) | lane
        packed_column = to_column(packed, eye)
        here = (packed_column >> 16) == lane_id
        meta[0:1, :] = jnp.sum(jnp.where(here, packed_column & 0xFFFF, 0), axis=0, keepdims=True)
        upto = jnp.sum((segment_column <= lane_id).astype(I32), axis=0, keepdims=True)
        count = jnp.sum((segment_column == lane_id).astype(I32), axis=0, keepdims=True)
        meta[1:2, :] = jnp.where(count > 0, upto - 1, NONE)
        local[1].wait()
        inverse = [jnp.full((1, BS), 64, I32), jnp.full((1, BS), 64, I32)]
        for n in range(64):
            place = left_s[0, n]
            for h in range(2):
                inverse[h] = jnp.where(lane + h * BS == place, n, inverse[h])
        meta[2:3, :] = inverse[0]
        meta[3:4, :] = inverse[1]
        copy = pltpu.make_async_copy(meta, meta_s, local_sem.at[8])
        copy.start()
        copy.wait()
        for copy in local[2:]:
            copy.wait()

    def stage_source(p):
        if p == 0:
            return
        yi, zi = SOURCES[p]
        a_tail = A_ROWS - 2 * BS
        b_head = BS - a_tail
        stage[4 * p] = gather_a[yi, zi, pl.ds(0, BS)]
        stage[4 * p + 1] = gather_a[yi, zi, pl.ds(BS, BS)]
        stage[4 * p + 2, pl.ds(0, a_tail)] = gather_a[yi, zi, pl.ds(2 * BS, a_tail)]
        stage[4 * p + 2, pl.ds(a_tail, b_head)] = gather_b[zi, yi, pl.ds(0, b_head)]
        stage[4 * p + 3] = gather_b[zi, yi, pl.ds(b_head, BS)]

    def multiply(start):
        for t in range(start, start + STEP):
            word = meta_s[0, t]
            block, slot, opens = word & 127, (word >> 7) & 255, word >> 15
            k, j = slot >> 3, slot & 7
            chosen = []
            for m in range(4):
                r = out_s[0, lax.rem(x + m, NX) * 8 + j] >> 3
                at = r * 32 + k
                chosen.append(left_set[meta_s[2 + (at >> 7), at & 127]])
            product = jnp.dot(
                jnp.concatenate(chosen, axis=0), stage[block], preferred_element_type=F32
            )
            previous = opens * NONE + (1 - opens) * (t - 1)
            products[t] = product + products[previous]

    def column_sum(target, jj, owner, first, last, fresh):
        ends = [meta_s[1, g * 8 + owner * 4 + jj] for g in range(first, last)]
        for m in range(4):
            rows = pl.ds(m * BS, BS)
            total = products[ends[0], rows] if fresh else target[jj, rows]
            for end in ends[1 if fresh else 0 :]:
                total = total + products[end, rows]
            target[jj, rows] = total

    def fold():
        for jj in range(4):
            column_sum(sib_send, jj, 1 - core, 0, FOLDED, True)
            column_sum(partial, jj, core, 0, FOLDED, True)

    def sib_copy(jj):
        return remote(SEND_SIB + jj, sib_send.at[jj], sib_recv.at[jj], sibling)

    left_set[64] = jnp.zeros((BS, BS), BF16)
    products[NONE] = jnp.zeros((ROWS, BS), F32)

    done = 0
    for item in PROGRAM:
        if item < 0:
            gather_copy(-1 - item).wait_recv()
        elif item < 200:
            gather_copy(item).start()
        elif item < 300:
            stage_source(item - 200)
        elif item == 300:
            multiply(done)
            done += STEP
        else:
            {400: sort_slots, 401: send_slots, 402: forward_slots, 500: fold}[item]()

    for jj in range(4):
        column_sum(sib_send, jj, 1 - core, FOLDED, NG, False)
        sib_copy(jj).start()
    for jj in range(4):
        column_sum(partial, jj, core, FOLDED, NG, False)

    half = BS // 2

    def x_copy(jj, what):
        number = SEND_X + jj * 6 + what
        forth = what % 2 == 0
        side = 0 if forth else 1
        device = along_xy(1, 0) if forth else along_xy(-1, 0)
        if what < 2:
            src = partial.at[jj, pl.ds(2 * BS + side * half, half)]
            dst = half_recv.at[side, jj]
        else:
            base = BS if forth else 3 * BS
            row = (half if forth else 0) if what < 4 else (0 if forth else half)
            src = partial.at[jj, pl.ds(base + row, half)]
            dst = full_recv.at[side, jj, pl.ds(row, half)]
        return remote(number, src, dst, device)

    for jj in range(4):
        sib_copy(jj).wait_recv()
        partial[jj] = partial[jj] + sib_recv[jj]
        x_copy(jj, 0).start()
        x_copy(jj, 1).start()
    for jj in range(4):
        x_copy(jj, 2).start()
        x_copy(jj, 3).start()
    for jj in range(4):
        x_copy(jj, 0).wait_recv()
        partial[jj, pl.ds(BS, half)] = partial[jj, pl.ds(BS, half)] + half_recv[0, jj]
        x_copy(jj, 4).start()
        x_copy(jj, 1).wait_recv()
        partial[jj, pl.ds(3 * BS + half, half)] = (
            partial[jj, pl.ds(3 * BS + half, half)] + half_recv[1, jj]
        )
        x_copy(jj, 5).start()
    stores = []
    for jj in range(4):
        for what in (2, 3, 4, 5):
            x_copy(jj, what).wait_recv()
        total = partial[jj, pl.ds(0, BS)] + full_recv[0, jj] + full_recv[1, jj]
        square = total * total
        squared[jj] = square
        stores.append(pltpu.make_async_copy(squared.at[jj], squares.at[jj], local_sem.at[9 + jj]))
        stores[-1].start()
        sums_xy[0, jj : jj + 1, :] = jnp.sum(square, axis=0, keepdims=True)

    def xy_copy(n):
        dx, dy = xy_peers[n]
        slot = ((-dx) % NX) * NY + (-dy) % NY
        return remote(SEND_SUM + n, sums_xy.at[0], sums_xy.at[slot], along_xy(dx, dy))

    def z_copy(n):
        d = (4, 3, 5, 2, 6, 1, 7)[n]
        return remote(SEND_SUM + 15 + n, sums_z.at[0], sums_z.at[(-d) % NZ], along_z(d))

    for n in range(15):
        xy_copy(n).start()
    total = sums_xy[0]
    for n in range(15):
        xy_copy(n).wait_recv()
    for n in range(1, 16):
        total = total + sums_xy[n]
    sums_z[0] = total
    for n in range(7):
        z_copy(n).start()
    for n in range(7):
        z_copy(n).wait_recv()
    for n in range(1, NZ):
        total = total + sums_z[n]
    meta_sum = sums_xy.at[1]
    meta_sum[...] = total / (NY * NZ * 4 * BS) + 1e-6
    last = pltpu.make_async_copy(meta_sum, sums, local_sem.at[13])
    last.start()

    for n in range(len(COPIES)):
        gather_copy(n).wait_send()
    for n in range(N_SMALL):
        small_copy(n).wait_send()
    for jj in range(4):
        sib_copy(jj).wait_send()
        for what in range(6):
            x_copy(jj, what).wait_send()
        stores[jj].wait()
    for n in range(15):
        xy_copy(n).wait_send()
    for n in range(7):
        z_copy(n).wait_send()
    last.wait()


def body(left_blocks, left_slots, right_blocks, right_slots, out_slots):
    any_spec = pl.BlockSpec(memory_space=pl.ANY)
    squares, sums = pl.pallas_call(
        kernel,
        out_shape=(
            jax.ShapeDtypeStruct((4, BS, BS), F32),
            jax.ShapeDtypeStruct((4, BS), F32),
        ),
        in_specs=[any_spec] * 5,
        out_specs=(any_spec, any_spec),
        scratch_shapes=[
            pltpu.VMEM((65, BS, BS), BF16),
            pltpu.VMEM((NY, NZ, A_ROWS, BS), BF16),
            pltpu.VMEM((NZ, NY, B_ROWS, BS), BF16),
            pltpu.VMEM((32 * 4, BS, BS), BF16),
            pltpu.VMEM((NONE + 1, ROWS, BS), F32),
            pltpu.VMEM((1, BS), I32),
            pltpu.VMEM((NY, NZ, 1, BS), I32),
            pltpu.VMEM((8, BS), I32),
            pltpu.SMEM((8, BS), I32),
            pltpu.SMEM((1, 64), I32),
            pltpu.SMEM((1, 4), I32),
            pltpu.SMEM((1, 32), I32),
            pltpu.VMEM((4, ROWS, BS), F32),
            pltpu.VMEM((4, ROWS, BS), F32),
            pltpu.VMEM((4, ROWS, BS), F32),
            pltpu.VMEM((2, 4, BS // 2, BS), F32),
            pltpu.VMEM((2, 4, BS, BS), F32),
            pltpu.VMEM((16, 4, BS), F32),
            pltpu.VMEM((NZ, 4, BS), F32),
            pltpu.VMEM((4, BS, BS), F32),
            pltpu.SemaphoreType.DMA((N_SEM,)),
            pltpu.SemaphoreType.DMA((N_SEM,)),
            pltpu.SemaphoreType.DMA((14,)),
        ],
        compiler_params=pltpu.CompilerParams(
            collective_id=0, has_side_effects=True, vmem_limit_bytes=60 * 2**20
        ),
        name="expand_and_sum",
    )(
        left_slots,
        right_slots,
        out_slots,
        left_blocks.reshape(64, BS, BS),
        right_blocks.reshape(ROWS, BS),
    )
    return (squares / sums[:, None, :])[None]


def solution(mesh):
    return jax.shard_map(
        body,
        mesh=mesh,
        in_specs=(
            P(("row", "col"), "layer", None, None),
            P(("row", "col"), "layer"),
            P("layer", ("row", "col"), None, None),
            P("layer", ("row", "col")),
            P(("row", "col"), None),
        ),
        out_specs=P(("row", "col"), "layer", None, None),
        check_vma=False,
    )
```

```python
import functools

import jax
import jax.numpy as jnp
from jax import lax
from jax.experimental import pallas as pl
from jax.experimental.pallas import tpu as pltpu
from jax.sharding import PartitionSpec as P

MESH = pl.DeviceIdType.MESH
F32 = jnp.float32
BF16 = jnp.bfloat16
I32 = jnp.int32

BS = 128
NY, NZ, NX = 4, 8, 4
ROWS = 4 * BS
A_ROWS, B_ROWS = 304, 208
A_CUT, B_CUT = 160, 96
Z_INDEX = {0: 0, 1: 1, -1: 2, 2: 3, -2: 4, 3: 5, -3: 6, 4: 7}
Y_INDEX = {0: 0, 1: 1, -1: 2, 2: 3}
SOURCES = (
    (0, 0), (1, 0), (0, 1), (0, 2), (2, 1), (2, 0), (1, 1), (0, 4), (1, 2), (2, 2), (0, 3), (3, 0),
    (3, 2), (3, 1), (2, 3), (1, 4), (2, 4), (1, 3), (0, 5), (0, 6), (3, 3), (3, 4), (2, 6), (2, 5),
    (1, 6), (1, 5), (0, 7), (1, 7), (3, 6), (3, 5), (2, 7), (3, 7),
)
GROUPS = (4, 6, 8, 4, 4, 2, 2, 2)
PROGRAMS = (
    (
        0, 13, 8, 200, 5, 999, 16, 20, 54, 48, -14, -15, 15, -6, -7, 7, 60, 89, -50, 65, -55, -56,
        -49, 91, -81, 999, -85, -16, -8, 70, 90, 56, 75, 50, 999, -61, -66, 66, 61, 94, -71, 200,
        200, -23, -86, -57, -19, 200, 999, 200, -82, 71, -51, 92, -76, 97, 999, 200, 200, 76, 200,
        200, 200, 51, 57, 999, 999, 200, 999, -29, -26, -87, 200, 200, 200, -62, 62, -67, 95, 200,
        67, 200, 200, 200, 999, -83, -72, -35, 999, 72, -77, 77, -32, -84, 98, 999, -52, -58, 93,
        52, 200, 200, 53, 200, 58, 200, 59, 999, 999, -63, 64, 63, -68, 96, 68, 999, 69, -73, 74,
        -88, -78, 73, -53, 78, -59, 79, 200, 200, 200, 200, 999, 999, 99, -41, 999, 200, -89, -69,
        -64, -38, -79, 200, 999, -47, 200, -44, 200, 200, -74, 200, 999, 999,
    ),
    (
        1, 999, 14, 6, 49, 9, 17, 21, 55, -9, -1, -2, 2, -10, 10, 27, 24, 999, 200, -21, -17, 84,
        -18, 22, 80, -11, -3, 81, 18, -22, 30, 33, -92, 3, 11, -28, -90, 200, -25, 29, 85, 25, 19,
        26, 200, 200, 28, 999, 999, -95, 23, 999, 200, -4, 200, -34, -12, 12, 34, -31, 4, 31, -93,
        86, 32, 200, -91, 200, -30, 39, -98, 200, 82, -20, 200, 36, 200, 35, 999, 999, 999, -24,
        -27, 200, 200, -13, -5, 45, 200, 83, 42, -33, -96, 200, 200, 200, 200, 999, 999, 999, 999,
        -99, -40, 40, -94, 200, 200, 41, -36, 200, 200, -37, 87, 37, 999, 38, 999, -46, -54, 47,
        -43, 46, 43, -60, -97, 200, 200, 200, 88, 200, 44, 999, 999, 999, -75, -42, -70, -100, 200,
        -48, -65, -39, 200, 200, -45, -80, 200, 200, 200, 999, 999, 999,
    ),
)
SHARED = (401, 402, 400) + (300,) * 13 + (500,) + (300,) * 3
STEP = 8
NG = len(GROUPS)
FOLDED = 5
NONE = 128


def wrap(value, count):
    value = value % count
    return value - count if value > count // 2 else value


def gather_copies():
    plans = {}

    def part(kind, sign, whole):
        size, cut = (A_ROWS, A_CUT) if kind == 0 else (B_ROWS, B_CUT)
        if whole:
            return 0, size
        return (0, cut) if sign == 1 else (cut, size - cut)

    def plan(key, kind, axis, sign, d, other, form):
        index, count = ((Y_INDEX, NY), (Z_INDEX, NZ))[axis]
        src = (index[-sign * (d - 1)], 1)
        dst = (index[wrap(-sign * d, count)], 1)
        first_axis = 0 if kind == 0 else 1
        order = (lambda v: (v, other)) if axis == first_axis else (lambda v: (other, v))
        plans[key] = dict(
            kind=kind, axis=axis, sign=sign, src=order(src), dst=order(dst),
            rows=part(kind, sign, d < count // 2), form=form,
        )

    for sign in (1, -1):
        for d in range(1, 5):
            plan(("Az", sign, d), 0, 1, sign, d, (0, 1), "own" if d == 1 else "pass")
        for d in (1, 2):
            plan(("By", sign, d), 1, 0, sign, d, (0, 1), "own" if d == 1 else "pass")
    a_waves = ((0, 1), (1, 2), (3, 2), (5, 2), (7, 1))
    b_waves = ((0, 1), (1, 2), (3, 1))
    for w, wave in enumerate(a_waves):
        for sign in (1, -1):
            for d in (1, 2):
                form = "last" if d == 2 else "pass" if w else "own"
                plan(("Ay", w, sign, d), 0, 0, sign, d, wave, form)
    for v, wave in enumerate(b_waves):
        for sign in (1, -1):
            for d in range(1, 5):
                form = "last" if d == 4 else "pass" if v or d > 1 else "own"
                plan(("Bz", v, sign, d), 1, 1, sign, d, wave, form)
    copies = []
    for p in plans.values():
        agent = 1 - p["kind"]
        if p["form"] == "own":
            copies += [dict(p, ex=c, rc=agent, lay=c) for c in (0, 1)]
        elif p["form"] == "last":
            copies += [dict(p, ex=agent, rc=c, lay=c) for c in (0, 1)]
        else:
            copies.append(dict(p, ex=agent, rc=agent, lay=2))

    def push(kind, where):
        agent = 1 - kind
        rows = (0, A_ROWS if kind == 0 else B_ROWS)
        copies.append(
            dict(kind=kind, src=where, dst=where, rows=rows, form="push", ex=agent, rc=1 - agent, lay=1 - agent)
        )

    for wave in a_waves[1:]:
        push(0, ((0, 1), wave))
    for wave in a_waves:
        push(0, ((1, 2), wave))
    push(1, ((0, 1), (1, 2)))
    push(1, ((0, 1), (3, 1)))
    for wave in b_waves:
        for first in (1, 3, 5):
            push(1, ((first, 2), wave))
    return copies


COPIES = gather_copies()
N_SMALL = 7 + 3
N_X = 4 * 6
N_SUM = 15 + 7
SEND_SMALL = len(COPIES)
SEND_SIB = SEND_SMALL + N_SMALL
SEND_X = SEND_SIB + 4
SEND_SUM = SEND_X + N_X
N_SEM = SEND_SUM + N_SUM


def to_column(row, eye):
    return jnp.sum(jnp.where(eye, jnp.broadcast_to(row, (BS, BS)), 0), axis=1, keepdims=True)


def kernel(
    left_slots, right_slots, out_slots, left, right, squares, sums,
    left_set, gather_a, gather_b, stage, products, slots_row, slots, meta, meta_s,
    left_s, right_s, out_s, sib_send, sib_recv, partial, half_send, near_send, full_send,
    half_recv, near_recv, full_recv,
    sums_xy, sums_z, squared, send_sem, recv_sem, local_sem,
):
    y, z, layer = lax.axis_index("row"), lax.axis_index("col"), lax.axis_index("layer")
    x, core = layer >> 1, layer & 1

    ys = [y] + [(y + d) & (NY - 1) for d in range(1, NY)]
    zs = [z] + [(z + d) & (NZ - 1) for d in range(1, NZ)]
    xs = [x] + [(x + d) & (NX - 1) for d in range(1, NX)]
    layers = [layer] + [xs[d] * 2 + core for d in range(1, NX)]

    def along_y(d):
        return (ys[d % NY], z, layer)

    def along_z(d):
        return (y, zs[d % NZ], layer)

    def along_xy(dx, dy):
        return (ys[dy % NY], z, layers[dx % NX])

    def at_core(device, c):
        return (device[0], device[1], x * 2 + c)

    sibling = (y, z, x * 2 + (1 - core))
    xy_peers = [(dx, dy) for dx in range(NX) for dy in range(NY) if dx or dy]
    xy_peers.sort(key=lambda p: -min(p[0], NX - p[0]) - min(p[1], NY - p[1]))

    local = [
        pltpu.make_async_copy(right_slots, right_s, local_sem.at[0]),
        pltpu.make_async_copy(left_slots, left_s, local_sem.at[1]),
        pltpu.make_async_copy(out_slots, out_s, local_sem.at[2]),
        pltpu.make_async_copy(left, left_set.at[pl.ds(0, 64)], local_sem.at[3]),
    ] + [
        pltpu.make_async_copy(right.at[pl.ds(q * BS, BS)], stage.at[q], local_sem.at[4 + q])
        for q in range(4)
    ]
    for copy in local:
        copy.start()

    barrier = pltpu.get_barrier_semaphore()
    peers = [along_z(d) for d in range(1, NZ)] + [along_y(d) for d in range(1, NY)]
    peers += [along_xy(1, 0), along_xy(-1, 0), sibling]
    peers += [at_core(p, 1 - core) for p in (along_z(1), along_z(-1), along_y(1), along_y(-1))]
    for peer in peers:
        pl.semaphore_signal(barrier, 1, device_id=peer, device_id_type=MESH)
    pl.semaphore_wait(barrier, len(peers))

    def remote(number, src, dst, device):
        return pltpu.make_async_remote_copy(
            src_ref=src, dst_ref=dst, send_sem=send_sem.at[number], recv_sem=recv_sem.at[number],
            device_id=device, device_id_type=MESH,
        )

    def gather_copy(n):
        copy = COPIES[n]
        buffer = (gather_a, gather_b)[copy["kind"]]
        row, rows = copy["rows"]

        def place(where):
            index = [first if count == 1 else pl.ds(first, count) for first, count in where]
            lay = pl.ds(0, 2) if copy["lay"] == 2 else copy["lay"]
            return buffer.at[index[0], index[1], lay, pl.ds(row, rows)]

        if copy["form"] == "push":
            device = sibling
        else:
            along = along_z if copy["axis"] else along_y
            device = at_core(along(copy["sign"]), copy["rc"])
        if copy["form"] == "own":
            source = right.at[pl.ds((0 if copy["kind"] == 0 else A_ROWS) + row, rows)]
        else:
            source = place(copy["src"])
        return remote(n, source, place(copy["dst"]), device)

    def small_copy(n):
        if n < 7:
            d = n + 1
            return remote(
                SEND_SMALL + n, slots.at[0, 0], slots.at[0, Z_INDEX[wrap(-d, NZ)]], along_z(d)
            )
        d = n - 6
        return remote(SEND_SMALL + n, slots.at[0], slots.at[Y_INDEX[wrap(-d, NY)]], along_y(d))

    lane = lax.broadcasted_iota(I32, (1, BS), 1)

    def send_slots():
        local[0].wait()
        row = jnp.zeros((1, BS), I32)
        for q in range(4):
            row = jnp.where((lane & 3) == q, right_s[0, q], row)
        slots[0, 0] = row
        for n in range(7):
            small_copy(n).start()

    def forward_slots():
        for n in range(7):
            small_copy(n).wait_recv()
        for n in range(7, N_SMALL):
            small_copy(n).start()

    def sort_slots():
        for n in range(7, N_SMALL):
            small_copy(n).wait_recv()
        row_id = lax.broadcasted_iota(I32, (BS, BS), 0)
        lane_id = lax.broadcasted_iota(I32, (BS, BS), 1)
        eye = row_id == lane_id
        slot = jnp.zeros((1, BS), I32)
        for p, (yi, zi) in enumerate(SOURCES):
            slot = jnp.where((lane >> 2) == p, slots[yi, zi], slot)
        group = jnp.zeros((1, BS), I32)
        first = 0
        for size in GROUPS[:-1]:
            first += size
            group = group + ((lane >> 2) >= first).astype(I32)
        segment = group * 8 + (slot & 7)
        key = segment * BS + lane
        key_column = to_column(key, eye)
        rank = jnp.sum((key_column < key).astype(I32), axis=0, keepdims=True)
        segment_column = key_column >> 7
        before = jnp.sum((segment_column < segment).astype(I32), axis=0, keepdims=True)
        opens = (before == rank).astype(I32)
        packed = (rank << 16) | (opens << 15) | (slot << 7) | lane
        packed_column = to_column(packed, eye)
        here = (packed_column >> 16) == lane_id
        meta[0:1, :] = jnp.sum(jnp.where(here, packed_column & 0xFFFF, 0), axis=0, keepdims=True)
        upto = jnp.sum((segment_column <= lane_id).astype(I32), axis=0, keepdims=True)
        count = jnp.sum((segment_column == lane_id).astype(I32), axis=0, keepdims=True)
        meta[1:2, :] = jnp.where(count > 0, upto - 1, NONE)
        local[1].wait()
        inverse = [jnp.full((1, BS), 64, I32), jnp.full((1, BS), 64, I32)]
        for n in range(64):
            place = left_s[0, n]
            for h in range(2):
                inverse[h] = jnp.where(lane + h * BS == place, n, inverse[h])
        meta[2:3, :] = inverse[0]
        meta[3:4, :] = inverse[1]
        copy = pltpu.make_async_copy(meta, meta_s, local_sem.at[8])
        copy.start()
        copy.wait()
        for copy in local[2:]:
            copy.wait()

    def stage_source(p, c):
        if p == 0:
            return
        yi, zi = SOURCES[p]
        a_tail = A_ROWS - 2 * BS
        b_head = BS - a_tail
        stage[4 * p] = gather_a[yi, zi, c, pl.ds(0, BS)]
        stage[4 * p + 1] = gather_a[yi, zi, c, pl.ds(BS, BS)]
        stage[4 * p + 2, pl.ds(0, a_tail)] = gather_a[yi, zi, c, pl.ds(2 * BS, a_tail)]
        stage[4 * p + 2, pl.ds(a_tail, b_head)] = gather_b[zi, yi, c, pl.ds(0, b_head)]
        stage[4 * p + 3] = gather_b[zi, yi, c, pl.ds(b_head, BS)]

    def multiply(start):
        for t in range(start, start + STEP):
            word = meta_s[0, t]
            block, slot, opens = word & 127, (word >> 7) & 255, word >> 15
            k, j = slot >> 3, slot & 7
            chosen = []
            for m in range(4):
                r = out_s[0, xs[m] * 8 + j] >> 3
                at = r * 32 + k
                chosen.append(left_set[meta_s[2 + (at >> 7), at & 127]])
            product = jnp.dot(
                jnp.concatenate(chosen, axis=0), stage[block], preferred_element_type=F32
            )
            previous = opens * NONE + (1 - opens) * (t - 1)
            products[t] = product + products[previous]

    def column_sum(target, jj, owner, first, last, fresh):
        ends = [meta_s[1, g * 8 + owner * 4 + jj] for g in range(first, last)]
        for m in range(4):
            rows = pl.ds(m * BS, BS)
            total = products[ends[0], rows] if fresh else target[jj, rows]
            for end in ends[1 if fresh else 0 :]:
                total = total + products[end, rows]
            target[jj, rows] = total

    def fold():
        for jj in range(4):
            column_sum(sib_send, jj, 1 - core, 0, FOLDED, True)
            column_sum(partial, jj, core, 0, FOLDED, True)

    def sib_copy(jj):
        return remote(SEND_SIB + jj, sib_send.at[jj], sib_recv.at[jj], sibling)

    left_set[64] = jnp.zeros((BS, BS), BF16)
    products[NONE] = jnp.zeros((ROWS, BS), F32)

    def run(items, staged, c):
        for item in items:
            if item == 200:
                stage_source(staged, c)
                staged += 1
            elif item < 0:
                gather_copy(-1 - item).wait_recv()
            else:
                gather_copy(item).start()

    def sections(c):
        found, items, staged = [], [], 0
        for item in PROGRAMS[c] + (999,):
            if item == 999:
                found.append((items, staged))
                staged += items.count(200)
                items = []
            else:
                items.append(item)
        return found

    done = 0
    for n, (first, second) in enumerate(zip(sections(0), sections(1))):
        if first[0]:
            pl.when(core == 0)(functools.partial(run, *first, 0))
        if second[0]:
            pl.when(core == 1)(functools.partial(run, *second, 1))
        if n == len(SHARED):
            break
        if SHARED[n] == 300:
            multiply(done)
            done += STEP
        else:
            {400: sort_slots, 401: send_slots, 402: forward_slots, 500: fold}[SHARED[n]]()

    for jj in range(4):
        column_sum(sib_send, jj, 1 - core, FOLDED, NG, False)
        sib_copy(jj).start()
    for jj in range(4):
        column_sum(partial, jj, core, FOLDED, NG, False)

    half = BS // 2

    def exponent(value):
        largest = jnp.max(jnp.abs(value), axis=0, keepdims=True)
        return jnp.ceil(jnp.log2(jnp.maximum(largest, 1e-30)))

    def encode(value, power):
        scaled = jnp.round(value * jnp.exp2(15.0 - power))
        return jnp.clip(scaled, -32767.0, 32767.0).astype(I32).astype(jnp.int16)

    def decode(code, power):
        return code.astype(I32).astype(F32) * jnp.exp2(power - 15.0)

    def powers(first, second):
        rows = [jnp.broadcast_to(p.astype(I32), (8, BS)) for p in (first, second)]
        return jnp.concatenate(rows, axis=0).astype(jnp.int16)

    def read_powers(ref, side, jj):
        rows = ref[side, jj, pl.ds(half, 16)].astype(I32).astype(F32)
        return rows[0:1], rows[8:9]

    def x_copy(jj, what):
        side, stage_of = what % 2, what // 2
        src = (half_send, near_send, full_send)[stage_of].at[side, jj]
        dst = (half_recv, near_recv, full_recv)[stage_of].at[side, jj]
        device = along_xy(1, 0) if side == 0 else along_xy(-1, 0)
        return remote(SEND_X + jj * 6 + what, src, dst, device)

    for jj in range(4):
        sib_copy(jj).wait_recv()
        partial[jj] = partial[jj] + sib_recv[jj]
        for side in range(2):
            far = partial[jj, pl.ds(2 * BS + side * half, half)]
            near = partial[jj, pl.ds((BS + half) if side == 0 else 3 * BS, half)]
            far_power, near_power = exponent(far), exponent(near)
            half_send[side, jj, pl.ds(0, half)] = encode(far, far_power)
            half_send[side, jj, pl.ds(half, 16)] = powers(far_power, near_power)
            x_copy(jj, side).start()
            near_send[side, jj] = encode(near, near_power)
    for jj in range(4):
        x_copy(jj, 2).start()
        x_copy(jj, 3).start()
    for jj in range(4):
        for side in range(2):
            x_copy(jj, side).wait_recv()
            power, _ = read_powers(half_recv, side, jj)
            own = partial[jj, pl.ds(BS if side == 0 else 3 * BS + half, half)]
            value = own + decode(half_recv[side, jj, pl.ds(0, half)], power)
            power = exponent(value)
            full_send[side, jj, pl.ds(0, half)] = encode(value, power)
            full_send[side, jj, pl.ds(half, 16)] = powers(power, power)
            x_copy(jj, 4 + side).start()
    stores = []
    for jj in range(4):
        for what in (2, 3, 4, 5):
            x_copy(jj, what).wait_recv()
        total = []
        for part in range(2):
            value = partial[jj, pl.ds(part * half, half)]
            _, power = read_powers(half_recv, 1 - part, jj)
            value = value + decode(near_recv[1 - part, jj], power)
            power, _ = read_powers(full_recv, part, jj)
            total.append(value + decode(full_recv[part, jj, pl.ds(0, half)], power))
        total = jnp.concatenate(total, axis=0)
        square = total * total
        squared[jj] = square
        stores.append(pltpu.make_async_copy(squared.at[jj], squares.at[jj], local_sem.at[9 + jj]))
        stores[-1].start()
        sums_xy[0, jj : jj + 1, :] = jnp.sum(square, axis=0, keepdims=True)

    def xy_copy(n):
        dx, dy = xy_peers[n]
        slot = ((-dx) % NX) * NY + (-dy) % NY
        return remote(SEND_SUM + n, sums_xy.at[0], sums_xy.at[slot], along_xy(dx, dy))

    def z_copy(n):
        d = (4, 3, 5, 2, 6, 1, 7)[n]
        return remote(SEND_SUM + 15 + n, sums_z.at[0], sums_z.at[(-d) % NZ], along_z(d))

    for n in range(15):
        xy_copy(n).start()
    total = sums_xy[0]
    for n in range(15):
        xy_copy(n).wait_recv()
    for n in range(1, 16):
        total = total + sums_xy[n]
    sums_z[0] = total
    for n in range(7):
        z_copy(n).start()
    for n in range(7):
        z_copy(n).wait_recv()
    for n in range(1, NZ):
        total = total + sums_z[n]
    meta_sum = sums_xy.at[1]
    meta_sum[...] = total / (NY * NZ * 4 * BS) + 1e-6
    last = pltpu.make_async_copy(meta_sum, sums, local_sem.at[13])
    last.start()

    def finish(c):
        for n, copy in enumerate(COPIES):
            if copy["ex"] == c:
                gather_copy(n).wait_send()

    pl.when(core == 0)(functools.partial(finish, 0))
    pl.when(core == 1)(functools.partial(finish, 1))
    for n in range(N_SMALL):
        small_copy(n).wait_send()
    for jj in range(4):
        sib_copy(jj).wait_send()
        for what in range(6):
            x_copy(jj, what).wait_send()
        stores[jj].wait()
    for n in range(15):
        xy_copy(n).wait_send()
    for n in range(7):
        z_copy(n).wait_send()
    last.wait()


def body(left_blocks, left_slots, right_blocks, right_slots, out_slots):
    any_spec = pl.BlockSpec(memory_space=pl.ANY)
    squares, sums = pl.pallas_call(
        kernel,
        out_shape=(
            jax.ShapeDtypeStruct((4, BS, BS), F32),
            jax.ShapeDtypeStruct((4, BS), F32),
        ),
        in_specs=[any_spec] * 5,
        out_specs=(any_spec, any_spec),
        scratch_shapes=[
            pltpu.VMEM((65, BS, BS), BF16),
            pltpu.VMEM((NY, NZ, 2, A_ROWS, BS), BF16),
            pltpu.VMEM((NZ, NY, 2, B_ROWS, BS), BF16),
            pltpu.VMEM((32 * 4, BS, BS), BF16),
            pltpu.VMEM((NONE + 1, ROWS, BS), F32),
            pltpu.VMEM((1, BS), I32),
            pltpu.VMEM((NY, NZ, 1, BS), I32),
            pltpu.VMEM((8, BS), I32),
            pltpu.SMEM((8, BS), I32),
            pltpu.SMEM((1, 64), I32),
            pltpu.SMEM((1, 4), I32),
            pltpu.SMEM((1, 32), I32),
            pltpu.VMEM((4, ROWS, BS), F32),
            pltpu.VMEM((4, ROWS, BS), F32),
            pltpu.VMEM((4, ROWS, BS), F32),
            pltpu.VMEM((2, 4, BS // 2 + 16, BS), jnp.int16),
            pltpu.VMEM((2, 4, BS // 2, BS), jnp.int16),
            pltpu.VMEM((2, 4, BS // 2 + 16, BS), jnp.int16),
            pltpu.VMEM((2, 4, BS // 2 + 16, BS), jnp.int16),
            pltpu.VMEM((2, 4, BS // 2, BS), jnp.int16),
            pltpu.VMEM((2, 4, BS // 2 + 16, BS), jnp.int16),
            pltpu.VMEM((16, 4, BS), F32),
            pltpu.VMEM((NZ, 4, BS), F32),
            pltpu.VMEM((4, BS, BS), F32),
            pltpu.SemaphoreType.DMA((N_SEM,)),
            pltpu.SemaphoreType.DMA((N_SEM,)),
            pltpu.SemaphoreType.DMA((14,)),
        ],
        compiler_params=pltpu.CompilerParams(
            collective_id=0, has_side_effects=True, vmem_limit_bytes=60 * 2**20
        ),
        name="expand_and_sum",
    )(
        left_slots,
        right_slots,
        out_slots,
        left_blocks.reshape(64, BS, BS),
        right_blocks.reshape(ROWS, BS),
    )
    return (squares / sums[:, None, :])[None]


def solution(mesh):
    return jax.shard_map(
        body,
        mesh=mesh,
        in_specs=(
            P(("row", "col"), "layer", None, None),
            P(("row", "col"), "layer"),
            P("layer", ("row", "col"), None, None),
            P("layer", ("row", "col")),
            P(("row", "col"), None),
        ),
        out_specs=P(("row", "col"), "layer", None, None),
        check_vma=False,
    )
```

```python
import functools

import jax
import jax.numpy as jnp
from jax import lax
from jax.experimental import pallas as pl
from jax.experimental.pallas import tpu as pltpu
from jax.sharding import PartitionSpec as P

MESH = pl.DeviceIdType.MESH
F32 = jnp.float32
BF16 = jnp.bfloat16
I32 = jnp.int32

BS = 128
NY, NZ, NX = 4, 8, 4
ROWS = 4 * BS
A_ROWS, B_ROWS = 304, 208
A_CUT, B_CUT = 160, 96
Z_INDEX = {0: 0, 1: 1, -1: 2, 2: 3, -2: 4, 3: 5, -3: 6, 4: 7}
Y_INDEX = {0: 0, 1: 1, -1: 2, 2: 3}
SOURCES = (
    (0, 0), (1, 0), (0, 1), (0, 2), (2, 1), (2, 0), (1, 1), (0, 4), (1, 2), (2, 2), (0, 3), (3, 0),
    (3, 2), (3, 1), (2, 3), (1, 4), (2, 4), (1, 3), (0, 5), (0, 6), (3, 3), (3, 4), (2, 6), (2, 5),
    (1, 6), (1, 5), (0, 7), (1, 7), (3, 6), (3, 5), (2, 7), (3, 7),
)
GROUPS = (4, 6, 8, 4, 4, 2, 2, 2)
PROGRAMS = (
    (
        0, 13, 8, 200, 5, 999, 16, 20, 54, 48, -14, -15, 15, -6, -7, 7, 60, 89, -50, 65, -55, -56,
        -49, 91, -81, 999, -85, -16, -8, 70, 90, 56, 75, 50, 999, -61, -66, 66, 61, 94, -71, 200,
        200, -23, -86, -57, -19, 200, 999, 200, -82, 71, -51, 92, -76, 97, 999, 200, 200, 76, 200,
        200, 200, 51, 57, 999, 999, 200, 999, -29, -26, -87, 200, 200, 200, -62, 62, -67, 95, 200,
        67, 200, 200, 200, 999, -83, -72, -35, 999, 72, -77, 77, -32, -84, 98, 999, -52, -58, 93,
        52, 200, 200, 53, 200, 58, 200, 59, 999, 999, -63, 64, 63, -68, 96, 68, 999, 69, -73, 74,
        -88, -78, 73, -53, 78, -59, 79, 200, 200, 200, 200, 999, 999, 99, -41, 999, 200, -89, -69,
        -64, -38, -79, 200, 999, -47, 200, -44, 200, 200, -74, 200, 999, 999,
    ),
    (
        1, 999, 14, 6, 49, 9, 17, 21, 55, -9, -1, -2, 2, -10, 10, 27, 24, 999, 200, -21, -17, 84,
        -18, 22, 80, -11, -3, 81, 18, -22, 30, 33, -92, 3, 11, -28, -90, 200, -25, 29, 85, 25, 19,
        26, 200, 200, 28, 999, 999, -95, 23, 999, 200, -4, 200, -34, -12, 12, 34, -31, 4, 31, -93,
        86, 32, 200, -91, 200, -30, 39, -98, 200, 82, -20, 200, 36, 200, 35, 999, 999, 999, -24,
        -27, 200, 200, -13, -5, 45, 200, 83, 42, -33, -96, 200, 200, 200, 200, 999, 999, 999, 999,
        -99, -40, 40, -94, 200, 200, 41, -36, 200, 200, -37, 87, 37, 999, 38, 999, -46, -54, 47,
        -43, 46, 43, -60, -97, 200, 200, 200, 88, 200, 44, 999, 999, 999, -75, -42, -70, -100, 200,
        -48, -65, -39, 200, 200, -45, -80, 200, 200, 200, 999, 999, 999,
    ),
)
SHARED = (401, 402, 400) + (300,) * 13 + (500,) + (300,) * 3
STEP = 8
NG = len(GROUPS)
FOLDED = 5
NONE = 128


def wrap(value, count):
    value = value % count
    return value - count if value > count // 2 else value


def gather_copies():
    plans = {}

    def part(kind, sign, whole):
        size, cut = (A_ROWS, A_CUT) if kind == 0 else (B_ROWS, B_CUT)
        if whole:
            return 0, size
        return (0, cut) if sign == 1 else (cut, size - cut)

    def plan(key, kind, axis, sign, d, other, form):
        index, count = ((Y_INDEX, NY), (Z_INDEX, NZ))[axis]
        src = (index[-sign * (d - 1)], 1)
        dst = (index[wrap(-sign * d, count)], 1)
        first_axis = 0 if kind == 0 else 1
        order = (lambda v: (v, other)) if axis == first_axis else (lambda v: (other, v))
        plans[key] = dict(
            kind=kind, axis=axis, sign=sign, src=order(src), dst=order(dst),
            rows=part(kind, sign, d < count // 2), form=form,
        )

    for sign in (1, -1):
        for d in range(1, 5):
            plan(("Az", sign, d), 0, 1, sign, d, (0, 1), "own" if d == 1 else "pass")
        for d in (1, 2):
            plan(("By", sign, d), 1, 0, sign, d, (0, 1), "own" if d == 1 else "pass")
    a_waves = ((0, 1), (1, 2), (3, 2), (5, 2), (7, 1))
    b_waves = ((0, 1), (1, 2), (3, 1))
    for w, wave in enumerate(a_waves):
        for sign in (1, -1):
            for d in (1, 2):
                form = "last" if d == 2 else "pass" if w else "own"
                plan(("Ay", w, sign, d), 0, 0, sign, d, wave, form)
    for v, wave in enumerate(b_waves):
        for sign in (1, -1):
            for d in range(1, 5):
                form = "last" if d == 4 else "pass" if v or d > 1 else "own"
                plan(("Bz", v, sign, d), 1, 1, sign, d, wave, form)
    copies = []
    for p in plans.values():
        agent = 1 - p["kind"]
        if p["form"] == "own":
            copies += [dict(p, ex=c, rc=agent, lay=c) for c in (0, 1)]
        elif p["form"] == "last":
            copies += [dict(p, ex=agent, rc=c, lay=c) for c in (0, 1)]
        else:
            copies.append(dict(p, ex=agent, rc=agent, lay=2))

    def push(kind, where):
        agent = 1 - kind
        rows = (0, A_ROWS if kind == 0 else B_ROWS)
        copies.append(
            dict(kind=kind, src=where, dst=where, rows=rows, form="push", ex=agent, rc=1 - agent, lay=1 - agent)
        )

    for wave in a_waves[1:]:
        push(0, ((0, 1), wave))
    for wave in a_waves:
        push(0, ((1, 2), wave))
    push(1, ((0, 1), (1, 2)))
    push(1, ((0, 1), (3, 1)))
    for wave in b_waves:
        for first in (1, 3, 5):
            push(1, ((first, 2), wave))
    return copies


COPIES = gather_copies()
N_SMALL = 7 + 3
N_X = 4 * 6
N_SUM = 2
SEND_SMALL = len(COPIES)
SEND_SIB = SEND_SMALL + N_SMALL
SEND_X = SEND_SIB + 4
SEND_SUM = SEND_X + N_X
N_SEM = SEND_SUM + N_SUM


def to_column(row, eye):
    return jnp.sum(jnp.where(eye, jnp.broadcast_to(row, (BS, BS)), 0), axis=1, keepdims=True)


def kernel(
    left_slots, right_slots, out_slots, left, right, squares, sums,
    left_set, gather_a, gather_b, stage, products_0, products_1, products_2, products_3, slots_row, slots, meta, meta_s,
    left_s, right_s, out_s, sib_send, sib_recv, partial, half_send, near_send, full_send,
    half_recv, near_recv, full_recv,
    sums_xy, sums_z, scale, squared, send_sem, recv_sem, local_sem,
):
    y, z, layer = lax.axis_index("row"), lax.axis_index("col"), lax.axis_index("layer")
    x, core = layer >> 1, layer & 1
    products = (products_0, products_1, products_2, products_3)

    ys = [y] + [(y + d) & (NY - 1) for d in range(1, NY)]
    zs = [z] + [(z + d) & (NZ - 1) for d in range(1, NZ)]
    xs = [x] + [(x + d) & (NX - 1) for d in range(1, NX)]
    layers = [layer] + [xs[d] * 2 + core for d in range(1, NX)]

    def along_y(d):
        return (ys[d % NY], z, layer)

    def along_z(d):
        return (y, zs[d % NZ], layer)

    def along_xy(dx, dy):
        return (ys[dy % NY], z, layers[dx % NX])

    def at_core(device, c):
        return (device[0], device[1], x * 2 + c)

    sibling = (y, z, x * 2 + (1 - core))
    xy_peers = [(dx, dy) for dx in range(NX) for dy in range(NY) if dx or dy]
    xy_peers.sort(key=lambda p: -min(p[0], NX - p[0]) - min(p[1], NY - p[1]))

    local = [
        pltpu.make_async_copy(right_slots, right_s, local_sem.at[0]),
        pltpu.make_async_copy(left_slots, left_s, local_sem.at[1]),
        pltpu.make_async_copy(out_slots, out_s, local_sem.at[2]),
        pltpu.make_async_copy(left, left_set.at[pl.ds(0, 64)], local_sem.at[3]),
    ] + [
        pltpu.make_async_copy(right.at[pl.ds(q * BS, BS)], stage.at[q], local_sem.at[4 + q])
        for q in range(4)
    ]
    for copy in local:
        copy.start()

    barrier = pltpu.get_barrier_semaphore()
    peers = [along_z(d) for d in range(1, NZ)] + [along_y(d) for d in range(1, NY)]
    peers += [along_xy(1, 0), along_xy(-1, 0), sibling]
    peers += [at_core(p, 1 - core) for p in (along_z(1), along_z(-1), along_y(1), along_y(-1))]
    for peer in peers:
        pl.semaphore_signal(barrier, 1, device_id=peer, device_id_type=MESH)
    pl.semaphore_wait(barrier, len(peers))

    def remote(number, src, dst, device):
        return pltpu.make_async_remote_copy(
            src_ref=src, dst_ref=dst, send_sem=send_sem.at[number], recv_sem=recv_sem.at[number],
            device_id=device, device_id_type=MESH,
        )

    def gather_copy(n):
        copy = COPIES[n]
        buffer = (gather_a, gather_b)[copy["kind"]]
        row, rows = copy["rows"]

        def place(where):
            index = [first if count == 1 else pl.ds(first, count) for first, count in where]
            lay = pl.ds(0, 2) if copy["lay"] == 2 else copy["lay"]
            return buffer.at[index[0], index[1], lay, pl.ds(row, rows)]

        if copy["form"] == "push":
            device = sibling
        else:
            along = along_z if copy["axis"] else along_y
            device = at_core(along(copy["sign"]), copy["rc"])
        if copy["form"] == "own":
            source = right.at[pl.ds((0 if copy["kind"] == 0 else A_ROWS) + row, rows)]
        else:
            source = place(copy["src"])
        return remote(n, source, place(copy["dst"]), device)

    def small_copy(n):
        if n < 7:
            d = n + 1
            return remote(
                SEND_SMALL + n, slots.at[0, 0], slots.at[0, Z_INDEX[wrap(-d, NZ)]], along_z(d)
            )
        d = n - 6
        return remote(SEND_SMALL + n, slots.at[0], slots.at[Y_INDEX[wrap(-d, NY)]], along_y(d))

    lane = lax.broadcasted_iota(I32, (1, BS), 1)

    def send_slots():
        local[0].wait()
        row = jnp.zeros((1, BS), I32)
        for q in range(4):
            row = jnp.where((lane & 3) == q, right_s[0, q], row)
        slots[0, 0] = row
        for n in range(7):
            small_copy(n).start()

    def forward_slots():
        for n in range(7):
            small_copy(n).wait_recv()
        for n in range(7, N_SMALL):
            small_copy(n).start()

    def sort_slots():
        for n in range(7, N_SMALL):
            small_copy(n).wait_recv()
        row_id = lax.broadcasted_iota(I32, (BS, BS), 0)
        lane_id = lax.broadcasted_iota(I32, (BS, BS), 1)
        eye = row_id == lane_id
        slot = jnp.zeros((1, BS), I32)
        for p, (yi, zi) in enumerate(SOURCES):
            slot = jnp.where((lane >> 2) == p, slots[yi, zi], slot)
        group = jnp.zeros((1, BS), I32)
        first = 0
        for size in GROUPS[:-1]:
            first += size
            group = group + ((lane >> 2) >= first).astype(I32)
        segment = group * 8 + (slot & 7)
        key = segment * BS + lane
        key_column = to_column(key, eye)
        rank = jnp.sum((key_column < key).astype(I32), axis=0, keepdims=True)
        segment_column = key_column >> 7
        before = jnp.sum((segment_column < segment).astype(I32), axis=0, keepdims=True)
        opens = (before == rank).astype(I32)
        packed = (rank << 16) | (opens << 15) | (slot << 7) | lane
        packed_column = to_column(packed, eye)
        here = (packed_column >> 16) == lane_id
        meta[0:1, :] = jnp.sum(jnp.where(here, packed_column & 0xFFFF, 0), axis=0, keepdims=True)
        upto = jnp.sum((segment_column <= lane_id).astype(I32), axis=0, keepdims=True)
        count = jnp.sum((segment_column == lane_id).astype(I32), axis=0, keepdims=True)
        meta[1:2, :] = jnp.where(count > 0, upto - 1, NONE)
        local[1].wait()
        inverse = [jnp.full((1, BS), 64, I32), jnp.full((1, BS), 64, I32)]
        for n in range(64):
            place = left_s[0, n]
            for h in range(2):
                inverse[h] = jnp.where(lane + h * BS == place, n, inverse[h])
        meta[2:3, :] = inverse[0]
        meta[3:4, :] = inverse[1]
        copy = pltpu.make_async_copy(meta, meta_s, local_sem.at[8])
        copy.start()
        copy.wait()
        for copy in local[2:]:
            copy.wait()

    def stage_source(p, c):
        if p == 0:
            return
        yi, zi = SOURCES[p]
        a_tail = A_ROWS - 2 * BS
        b_head = BS - a_tail
        stage[4 * p] = gather_a[yi, zi, c, pl.ds(0, BS)]
        stage[4 * p + 1] = gather_a[yi, zi, c, pl.ds(BS, BS)]
        stage[4 * p + 2, pl.ds(0, a_tail)] = gather_a[yi, zi, c, pl.ds(2 * BS, a_tail)]
        stage[4 * p + 2, pl.ds(a_tail, b_head)] = gather_b[zi, yi, c, pl.ds(0, b_head)]
        stage[4 * p + 3] = gather_b[zi, yi, c, pl.ds(b_head, BS)]

    def multiply(start):
        for t in range(start, start + STEP):
            word = meta_s[0, t]
            block, slot, opens = word & 127, (word >> 7) & 255, word >> 15
            k, j = slot >> 3, slot & 7
            chosen = []
            for m in range(4):
                r = out_s[0, xs[m] * 8 + j] >> 3
                at = r * 32 + k
                chosen.append(left_set[meta_s[2 + (at >> 7), at & 127]])
            product = jnp.dot(
                jnp.concatenate(chosen, axis=0), stage[block], preferred_element_type=F32
            )
            previous = opens * NONE + (1 - opens) * (t - 1)
            for m in range(4):
                rows = product[m * BS : (m + 1) * BS]
                products[m][t] = rows + products[m][previous]

    def column_sum(target, jj, owner, first, last, fresh):
        ends = [meta_s[1, g * 8 + owner * 4 + jj] for g in range(first, last)]
        for m in range(4):
            rows = pl.ds(m * BS, BS)
            total = products[m][ends[0]] if fresh else target[jj, rows]
            for end in ends[1 if fresh else 0 :]:
                total = total + products[m][end]
            target[jj, rows] = total

    def fold():
        for jj in range(4):
            column_sum(sib_send, jj, 1 - core, 0, FOLDED, True)
            column_sum(partial, jj, core, 0, FOLDED, True)

    def sib_copy(jj):
        return remote(SEND_SIB + jj, sib_send.at[jj], sib_recv.at[jj], sibling)

    left_set[64] = jnp.zeros((BS, BS), BF16)
    for m in range(4):
        products[m][NONE] = jnp.zeros((BS, BS), F32)

    def run(items, staged, c):
        for item in items:
            if item == 200:
                stage_source(staged, c)
                staged += 1
            elif item < 0:
                gather_copy(-1 - item).wait_recv()
            else:
                gather_copy(item).start()

    def sections(c):
        found, items, staged = [], [], 0
        for item in PROGRAMS[c] + (999,):
            if item == 999:
                found.append((items, staged))
                staged += items.count(200)
                items = []
            else:
                items.append(item)
        return found

    done = 0
    for n, (first, second) in enumerate(zip(sections(0), sections(1))):
        if first[0]:
            pl.when(core == 0)(functools.partial(run, *first, 0))
        if second[0]:
            pl.when(core == 1)(functools.partial(run, *second, 1))
        if n == len(SHARED):
            break
        if SHARED[n] == 300:
            multiply(done)
            done += STEP
        else:
            {400: sort_slots, 401: send_slots, 402: forward_slots, 500: fold}[SHARED[n]]()

    for jj in range(4):
        column_sum(sib_send, jj, 1 - core, FOLDED, NG, False)
        sib_copy(jj).start()
    for jj in range(4):
        column_sum(partial, jj, core, FOLDED, NG, False)

    half = BS // 2

    def exponent(value):
        largest = jnp.max(jnp.abs(value), axis=0, keepdims=True)
        return jnp.ceil(jnp.log2(jnp.maximum(largest, 1e-30)))

    def encode(value, power):
        scaled = jnp.round(value * jnp.exp2(15.0 - power))
        return jnp.clip(scaled, -32767.0, 32767.0).astype(I32).astype(jnp.int16)

    def decode(code, power):
        return code.astype(I32).astype(F32) * jnp.exp2(power - 15.0)

    def powers(first, second):
        rows = [jnp.broadcast_to(p.astype(I32), (8, BS)) for p in (first, second)]
        return jnp.concatenate(rows, axis=0).astype(jnp.int16)

    def read_powers(ref, side, jj):
        rows = ref[side, jj, pl.ds(half, 16)].astype(I32).astype(F32)
        return rows[0:1], rows[8:9]

    def drain(c, first, last):
        sent = [n for n, copy in enumerate(COPIES) if copy["ex"] == c]
        for n in sent[first:last]:
            gather_copy(n).wait_send()

    def drain_gather(first, last):
        pl.when(core == 0)(functools.partial(drain, 0, first, last))
        pl.when(core == 1)(functools.partial(drain, 1, first, last))

    def x_copy(jj, what):
        side, stage_of = what % 2, what // 2
        src = (half_send, near_send, full_send)[stage_of].at[side, jj]
        dst = (half_recv, near_recv, full_recv)[stage_of].at[side, jj]
        device = along_xy(1, 0) if side == 0 else along_xy(-1, 0)
        return remote(SEND_X + jj * 6 + what, src, dst, device)

    drain_gather(0, 16)
    for jj in range(4):
        sib_copy(jj).wait_recv()
        partial[jj] = partial[jj] + sib_recv[jj]
        for side in range(2):
            far = partial[jj, pl.ds(2 * BS + side * half, half)]
            near = partial[jj, pl.ds((BS + half) if side == 0 else 3 * BS, half)]
            far_power, near_power = exponent(far), exponent(near)
            half_send[side, jj, pl.ds(0, half)] = encode(far, far_power)
            half_send[side, jj, pl.ds(half, 16)] = powers(far_power, near_power)
            x_copy(jj, side).start()
            near_send[side, jj] = encode(near, near_power)
    for jj in range(4):
        x_copy(jj, 2).start()
        x_copy(jj, 3).start()
    drain_gather(16, len(COPIES))
    for jj in range(4):
        for side in range(2):
            x_copy(jj, side).wait_recv()
            power, _ = read_powers(half_recv, side, jj)
            own = partial[jj, pl.ds(BS if side == 0 else 3 * BS + half, half)]
            value = own + decode(half_recv[side, jj, pl.ds(0, half)], power)
            power = exponent(value)
            full_send[side, jj, pl.ds(0, half)] = encode(value, power)
            full_send[side, jj, pl.ds(half, 16)] = powers(power, power)
            x_copy(jj, 4 + side).start()
    for n in range(N_SMALL):
        small_copy(n).wait_send()
    for jj in range(4):
        sib_copy(jj).wait_send()
        for what in range(4):
            x_copy(jj, what).wait_send()
    stores = []
    for jj in range(4):
        for what in (2, 3, 4, 5):
            x_copy(jj, what).wait_recv()
        total = []
        for part in range(2):
            value = partial[jj, pl.ds(part * half, half)]
            _, power = read_powers(half_recv, 1 - part, jj)
            value = value + decode(near_recv[1 - part, jj], power)
            power, _ = read_powers(full_recv, part, jj)
            total.append(value + decode(full_recv[part, jj, pl.ds(0, half)], power))
        total = jnp.concatenate(total, axis=0)
        square = total * total
        squared[jj] = square
        stores.append(pltpu.make_async_copy(squared.at[jj], squares.at[jj], local_sem.at[9 + jj]))
        stores[-1].start()
        sums_xy[0, jj : jj + 1, :] = jnp.sum(square, axis=0, keepdims=True)

    def xy_copy(n):
        dx, dy = xy_peers[n]
        slot = ((-dx) % NX) * NY + (-dy) % NY
        return remote(SEND_SUM, sums_xy.at[0], sums_xy.at[slot], along_xy(dx, dy))

    def z_copy(n):
        d = (4, 3, 5, 2, 6, 1, 7)[n]
        return remote(SEND_SUM + 1, sums_z.at[0], sums_z.at[(-d) % NZ], along_z(d))

    xy_all = sums_xy.at[pl.ds(1, 15)]
    z_all = sums_z.at[pl.ds(1, 7)]
    xy_round = remote(SEND_SUM, xy_all, xy_all, along_xy(1, 0))
    z_round = remote(SEND_SUM + 1, z_all, z_all, along_z(1))
    for n in range(15):
        xy_copy(n).start()
    total = sums_xy[0]
    for jj in range(4):
        x_copy(jj, 4).wait_send()
        x_copy(jj, 5).wait_send()
        stores[jj].wait()
    xy_round.wait_recv()
    for n in range(1, 16):
        total = total + sums_xy[n]
    sums_z[0] = total
    for n in range(7):
        z_copy(n).start()
    xy_round.wait_send()
    z_round.wait_recv()
    for n in range(1, NZ):
        total = total + sums_z[n]
    scale[...] = total / (NY * NZ * 4 * BS) + 1e-6
    last = pltpu.make_async_copy(scale, sums, local_sem.at[13])
    last.start()
    z_round.wait_send()
    last.wait()


def body(left_blocks, left_slots, right_blocks, right_slots, out_slots):
    any_spec = pl.BlockSpec(memory_space=pl.ANY)
    squares, sums = pl.pallas_call(
        kernel,
        out_shape=(
            jax.ShapeDtypeStruct((4, BS, BS), F32),
            jax.ShapeDtypeStruct((4, BS), F32),
        ),
        in_specs=[any_spec] * 5,
        out_specs=(any_spec, any_spec),
        scratch_shapes=[
            pltpu.VMEM((65, BS, BS), BF16),
            pltpu.VMEM((NY, NZ, 2, A_ROWS, BS), BF16),
            pltpu.VMEM((NZ, NY, 2, B_ROWS, BS), BF16),
            pltpu.VMEM((32 * 4, BS, BS), BF16),
            pltpu.VMEM((NONE + 1, BS, BS), F32),
            pltpu.VMEM((NONE + 1, BS, BS), F32),
            pltpu.VMEM((NONE + 1, BS, BS), F32),
            pltpu.VMEM((NONE + 1, BS, BS), F32),
            pltpu.VMEM((1, BS), I32),
            pltpu.VMEM((NY, NZ, 1, BS), I32),
            pltpu.VMEM((8, BS), I32),
            pltpu.SMEM((8, BS), I32),
            pltpu.SMEM((1, 64), I32),
            pltpu.SMEM((1, 4), I32),
            pltpu.SMEM((1, 32), I32),
            pltpu.VMEM((4, ROWS, BS), F32),
            pltpu.VMEM((4, ROWS, BS), F32),
            pltpu.VMEM((4, ROWS, BS), F32),
            pltpu.VMEM((2, 4, BS // 2 + 16, BS), jnp.int16),
            pltpu.VMEM((2, 4, BS // 2, BS), jnp.int16),
            pltpu.VMEM((2, 4, BS // 2 + 16, BS), jnp.int16),
            pltpu.VMEM((2, 4, BS // 2 + 16, BS), jnp.int16),
            pltpu.VMEM((2, 4, BS // 2, BS), jnp.int16),
            pltpu.VMEM((2, 4, BS // 2 + 16, BS), jnp.int16),
            pltpu.VMEM((16, 4, BS), F32),
            pltpu.VMEM((NZ, 4, BS), F32),
            pltpu.VMEM((4, BS), F32),
            pltpu.VMEM((4, BS, BS), F32),
            pltpu.SemaphoreType.DMA((N_SEM,)),
            pltpu.SemaphoreType.DMA((N_SEM,)),
            pltpu.SemaphoreType.DMA((14,)),
        ],
        compiler_params=pltpu.CompilerParams(
            collective_id=0, has_side_effects=True, vmem_limit_bytes=60 * 2**20
        ),
        name="expand_and_sum",
    )(
        left_slots,
        right_slots,
        out_slots,
        left_blocks.reshape(64, BS, BS),
        right_blocks.reshape(ROWS, BS),
    )
    return (squares / sums[:, None, :])[None]


def solution(mesh):
    return jax.shard_map(
        body,
        mesh=mesh,
        in_specs=(
            P(("row", "col"), "layer", None, None),
            P(("row", "col"), "layer"),
            P("layer", ("row", "col"), None, None),
            P("layer", ("row", "col")),
            P(("row", "col"), None),
        ),
        out_specs=P(("row", "col"), "layer", None, None),
        check_vma=False,
    )
```

```python
import functools

import jax
import jax.numpy as jnp
from jax import lax
from jax.experimental import pallas as pl
from jax.experimental.pallas import tpu as pltpu
from jax.sharding import PartitionSpec as P

MESH = pl.DeviceIdType.MESH
F32 = jnp.float32
BF16 = jnp.bfloat16
I32 = jnp.int32

BS = 128
NY, NZ, NX = 4, 8, 4
ROWS = 4 * BS
A_ROWS, B_ROWS = 304, 208
A_CUT, B_CUT = 160, 96
Z_INDEX = {0: 0, 1: 1, -1: 2, 2: 3, -2: 4, 3: 5, -3: 6, 4: 7}
Y_INDEX = {0: 0, 1: 1, -1: 2, 2: 3}
SOURCES = (
    (0, 0), (1, 2), (2, 2), (2, 1), (1, 0), (0, 1), (2, 0), (0, 2), (0, 3), (0, 4), (1, 1), (3, 1),
    (3, 0), (1, 3), (2, 4), (3, 2), (1, 4), (2, 3), (0, 6), (0, 5), (3, 3), (3, 4), (2, 5), (2, 6),
    (1, 6), (1, 5), (0, 7), (3, 6), (3, 5), (2, 7), (1, 7), (3, 7),
)
GROUPS = (4, 6, 8, 4, 4, 2, 2, 2)
PROGRAMS = (
    (
        8, 5, 0, 13, 54, 999, 48, 16, 20, -6, -7, 7, -14, -15, 15, 65, 999, 89, 60, -56, -8, -50,
        91, -55, -49, -16, 50, 56, 70, 75, -81, -66, -61, 61, 94, 200, 66, -23, -82, -85, 90, -51,
        -19, -57, 999, -86, 51, 200, 200, 200, 57, -76, -71, 97, 92, 200, 76, 200, 200, 200, 999,
        71, 200, 999, 200, 200, -87, 999, -29, 999, -26, -67, 67, 200, 200, -62, 62, 95, 200, 999,
        -83, -58, 200, 200, -52, 93, 200, 200, 200, 999, -32, -77, 77, 59, -72, 72, -35, 58, 98,
        200, 200, 53, 52, 200, 999, 999, -84, 999, 999, -68, 68, 69, -63, 96, 64, 63, -88, 999, -78,
        79, 200, 200, 78, 200, 200, -73, 73, 99, 74, -53, 999, 999, -41, -59, -89, 999, -69, -38,
        200, 200, 999, -44, -64, 200, 200, 200, -47, -74, -79, 999, 200, 999,
    ),
    (
        9, 999, 6, 1, 14, 200, 49, 55, 17, 21, -9, -10, 10, -1, -2, 2, 24, 27, -17, 80, -22, -21,
        84, 999, -11, 18, -18, -3, 30, 22, 3, 33, 11, -25, 81, 23, -28, 28, 19, 26, 85, -95, 29,
        200, 25, -92, 999, -12, -31, 200, -4, 31, -34, 34, 86, 36, 12, 200, -90, 39, 82, 999, -98,
        200, 200, 35, 32, 4, -93, 200, 200, 999, -27, -30, -24, 200, -91, 200, 999, 200, 999, -20,
        200, 200, 999, -96, 200, 200, 200, 200, 200, 999, -5, -13, 42, 45, 83, -94, 999, 999, 200,
        -37, -40, 40, 87, 999, 41, -33, -36, 38, -99, 200, 37, 200, 200, 999, 999, -60, -54, -43,
        43, 44, -46, 47, 46, -97, 88, 200, 200, 200, 200, 999, 999, 999, -39, -100, 200, -42, 200,
        999, -48, -45, -65, 200, -70, -75, -80, 200, 200, 999, 200, 999,
    ),
)
SHARED = (401, 402, 400) + (300,) * 13 + (500,) + (300,) * 3
STEP = 8
NG = len(GROUPS)
FOLDED = 5
NONE = 128


def wrap(value, count):
    value = value % count
    return value - count if value > count // 2 else value


def gather_copies():
    plans = {}

    def part(kind, sign, whole):
        size, cut = (A_ROWS, A_CUT) if kind == 0 else (B_ROWS, B_CUT)
        if whole:
            return 0, size
        return (0, cut) if sign == 1 else (cut, size - cut)

    def plan(key, kind, axis, sign, d, other, form):
        index, count = ((Y_INDEX, NY), (Z_INDEX, NZ))[axis]
        src = (index[-sign * (d - 1)], 1)
        dst = (index[wrap(-sign * d, count)], 1)
        first_axis = 0 if kind == 0 else 1
        order = (lambda v: (v, other)) if axis == first_axis else (lambda v: (other, v))
        plans[key] = dict(
            kind=kind, axis=axis, sign=sign, src=order(src), dst=order(dst),
            rows=part(kind, sign, d < count // 2), form=form,
        )

    for sign in (1, -1):
        for d in range(1, 5):
            plan(("Az", sign, d), 0, 1, sign, d, (0, 1), "own" if d == 1 else "pass")
        for d in (1, 2):
            plan(("By", sign, d), 1, 0, sign, d, (0, 1), "own" if d == 1 else "pass")
    a_waves = ((0, 1), (1, 2), (3, 2), (5, 2), (7, 1))
    b_waves = ((0, 1), (1, 2), (3, 1))
    for w, wave in enumerate(a_waves):
        for sign in (1, -1):
            for d in (1, 2):
                form = "last" if d == 2 else "pass" if w else "own"
                plan(("Ay", w, sign, d), 0, 0, sign, d, wave, form)
    for v, wave in enumerate(b_waves):
        for sign in (1, -1):
            for d in range(1, 5):
                form = "last" if d == 4 else "pass" if v or d > 1 else "own"
                plan(("Bz", v, sign, d), 1, 1, sign, d, wave, form)
    copies = []
    for p in plans.values():
        agent = 1 - p["kind"]
        if p["form"] == "own":
            copies += [dict(p, ex=c, rc=agent, lay=c) for c in (0, 1)]
        elif p["form"] == "last":
            copies += [dict(p, ex=agent, rc=c, lay=c) for c in (0, 1)]
        else:
            copies.append(dict(p, ex=agent, rc=agent, lay=2))

    def push(kind, where):
        agent = 1 - kind
        rows = (0, A_ROWS if kind == 0 else B_ROWS)
        copies.append(
            dict(kind=kind, src=where, dst=where, rows=rows, form="push", ex=agent, rc=1 - agent, lay=1 - agent)
        )

    for wave in a_waves[1:]:
        push(0, ((0, 1), wave))
    for wave in a_waves:
        push(0, ((1, 2), wave))
    push(1, ((0, 1), (1, 2)))
    push(1, ((0, 1), (3, 1)))
    for wave in b_waves:
        for first in (1, 3, 5):
            push(1, ((first, 2), wave))
    return copies


COPIES = gather_copies()
N_SMALL = 7 + 3
N_X = 4 * 6
N_SUM = 2
SEND_SMALL = len(COPIES)
SEND_SIB = SEND_SMALL + N_SMALL
SEND_X = SEND_SIB + 4
SEND_SUM = SEND_X + N_X
N_SEM = SEND_SUM + N_SUM


def to_column(row, eye):
    return jnp.sum(jnp.where(eye, jnp.broadcast_to(row, (BS, BS)), 0), axis=1, keepdims=True)


def kernel(
    left_slots, right_slots, out_slots, left, right, squares, sums,
    left_set, gather_a, gather_b, stage, products_0, products_1, products_2, products_3, slots_row, slots, meta, meta_s,
    left_s, right_s, out_s, sib_send, sib_recv, partial, half_send, near_send, full_send,
    half_recv, near_recv, full_recv,
    sums_xy, sums_z, scale, squared, send_sem, recv_sem, local_sem,
):
    y, z, layer = lax.axis_index("row"), lax.axis_index("col"), lax.axis_index("layer")
    x, core = layer >> 1, layer & 1
    products = (products_0, products_1, products_2, products_3)

    ys = [y] + [(y + d) & (NY - 1) for d in range(1, NY)]
    zs = [z] + [(z + d) & (NZ - 1) for d in range(1, NZ)]
    xs = [x] + [(x + d) & (NX - 1) for d in range(1, NX)]
    layers = [layer] + [xs[d] * 2 + core for d in range(1, NX)]

    def along_y(d):
        return (ys[d % NY], z, layer)

    def along_z(d):
        return (y, zs[d % NZ], layer)

    def along_xy(dx, dy):
        return (ys[dy % NY], z, layers[dx % NX])

    def at_core(device, c):
        return (device[0], device[1], x * 2 + c)

    sibling = (y, z, x * 2 + (1 - core))
    xy_peers = [(dx, dy) for dx in range(NX) for dy in range(NY) if dx or dy]
    xy_peers.sort(key=lambda p: -min(p[0], NX - p[0]) - min(p[1], NY - p[1]))

    barrier = pltpu.get_barrier_semaphore()
    peers = [along_z(d) for d in (4, 3, 5, 2, 6, 1, 7)] + [along_y(d) for d in (2, 1, 3)]
    peers += [along_xy(1, 0), along_xy(-1, 0), sibling]
    peers += [at_core(p, 1 - core) for p in (along_z(1), along_z(-1), along_y(1), along_y(-1))]
    for peer in peers:
        pl.semaphore_signal(barrier, 1, device_id=peer, device_id_type=MESH)
    local = [
        pltpu.make_async_copy(right_slots, right_s, local_sem.at[0]),
        pltpu.make_async_copy(left_slots, left_s, local_sem.at[1]),
        pltpu.make_async_copy(out_slots, out_s, local_sem.at[2]),
        pltpu.make_async_copy(left, left_set.at[pl.ds(0, 64)], local_sem.at[3]),
    ] + [
        pltpu.make_async_copy(right.at[pl.ds(q * BS, BS)], stage.at[q], local_sem.at[4 + q])
        for q in range(4)
    ]
    for copy in local:
        copy.start()
    left_set[64] = jnp.zeros((BS, BS), BF16)
    for m in range(4):
        products[m][NONE] = jnp.zeros((BS, BS), F32)
    pl.semaphore_wait(barrier, len(peers))

    def remote(number, src, dst, device):
        return pltpu.make_async_remote_copy(
            src_ref=src, dst_ref=dst, send_sem=send_sem.at[number], recv_sem=recv_sem.at[number],
            device_id=device, device_id_type=MESH,
        )

    def gather_copy(n):
        copy = COPIES[n]
        buffer = (gather_a, gather_b)[copy["kind"]]
        row, rows = copy["rows"]

        def place(where):
            index = [first if count == 1 else pl.ds(first, count) for first, count in where]
            lay = pl.ds(0, 2) if copy["lay"] == 2 else copy["lay"]
            return buffer.at[index[0], index[1], lay, pl.ds(row, rows)]

        if copy["form"] == "push":
            device = sibling
        else:
            along = along_z if copy["axis"] else along_y
            device = at_core(along(copy["sign"]), copy["rc"])
        if copy["form"] == "own":
            source = right.at[pl.ds((0 if copy["kind"] == 0 else A_ROWS) + row, rows)]
        else:
            source = place(copy["src"])
        return remote(n, source, place(copy["dst"]), device)

    def small_copy(n):
        if n < 7:
            d = n + 1
            return remote(
                SEND_SMALL + n, slots.at[0, 0], slots.at[0, Z_INDEX[wrap(-d, NZ)]], along_z(d)
            )
        d = n - 6
        return remote(SEND_SMALL + n, slots.at[0], slots.at[Y_INDEX[wrap(-d, NY)]], along_y(d))

    lane = lax.broadcasted_iota(I32, (1, BS), 1)

    def send_slots():
        local[0].wait()
        row = jnp.zeros((1, BS), I32)
        for q in range(4):
            row = jnp.where((lane & 3) == q, right_s[0, q], row)
        slots[0, 0] = row
        for n in range(7):
            small_copy(n).start()

    def forward_slots():
        for n in range(7):
            small_copy(n).wait_recv()
        for n in range(7, N_SMALL):
            small_copy(n).start()

    def sort_slots():
        for n in range(7, N_SMALL):
            small_copy(n).wait_recv()
        row_id = lax.broadcasted_iota(I32, (BS, BS), 0)
        lane_id = lax.broadcasted_iota(I32, (BS, BS), 1)
        eye = row_id == lane_id
        slot = jnp.zeros((1, BS), I32)
        for p, (yi, zi) in enumerate(SOURCES):
            slot = jnp.where((lane >> 2) == p, slots[yi, zi], slot)
        group = jnp.zeros((1, BS), I32)
        first = 0
        for size in GROUPS[:-1]:
            first += size
            group = group + ((lane >> 2) >= first).astype(I32)
        segment = group * 8 + (slot & 7)
        key = segment * BS + lane
        key_column = to_column(key, eye)
        rank = jnp.sum((key_column < key).astype(I32), axis=0, keepdims=True)
        segment_column = key_column >> 7
        before = jnp.sum((segment_column < segment).astype(I32), axis=0, keepdims=True)
        opens = (before == rank).astype(I32)
        packed = (rank << 16) | (opens << 15) | (slot << 7) | lane
        packed_column = to_column(packed, eye)
        here = (packed_column >> 16) == lane_id
        meta[0:1, :] = jnp.sum(jnp.where(here, packed_column & 0xFFFF, 0), axis=0, keepdims=True)
        upto = jnp.sum((segment_column <= lane_id).astype(I32), axis=0, keepdims=True)
        count = jnp.sum((segment_column == lane_id).astype(I32), axis=0, keepdims=True)
        meta[1:2, :] = jnp.where(count > 0, upto - 1, NONE)
        local[1].wait()
        inverse = [jnp.full((1, BS), 64, I32), jnp.full((1, BS), 64, I32)]
        for n in range(64):
            place = left_s[0, n]
            for h in range(2):
                inverse[h] = jnp.where(lane + h * BS == place, n, inverse[h])
        meta[2:3, :] = inverse[0]
        meta[3:4, :] = inverse[1]
        copy = pltpu.make_async_copy(meta, meta_s, local_sem.at[8])
        copy.start()
        copy.wait()
        for copy in local[2:]:
            copy.wait()

    def stage_source(p, c):
        if p == 0:
            return
        yi, zi = SOURCES[p]
        a_tail = A_ROWS - 2 * BS
        b_head = BS - a_tail
        stage[4 * p] = gather_a[yi, zi, c, pl.ds(0, BS)]
        stage[4 * p + 1] = gather_a[yi, zi, c, pl.ds(BS, BS)]
        stage[4 * p + 2, pl.ds(0, a_tail)] = gather_a[yi, zi, c, pl.ds(2 * BS, a_tail)]
        stage[4 * p + 2, pl.ds(a_tail, b_head)] = gather_b[zi, yi, c, pl.ds(0, b_head)]
        stage[4 * p + 3] = gather_b[zi, yi, c, pl.ds(b_head, BS)]

    def multiply(start):
        for t in range(start, start + STEP):
            word = meta_s[0, t]
            block, slot, opens = word & 127, (word >> 7) & 255, word >> 15
            k, j = slot >> 3, slot & 7
            chosen = []
            for m in range(4):
                r = out_s[0, xs[m] * 8 + j] >> 3
                at = r * 32 + k
                chosen.append(left_set[meta_s[2 + (at >> 7), at & 127]])
            product = jnp.dot(
                jnp.concatenate(chosen, axis=0), stage[block], preferred_element_type=F32
            )
            previous = opens * NONE + (1 - opens) * (t - 1)
            for m in range(4):
                rows = product[m * BS : (m + 1) * BS]
                products[m][t] = rows + products[m][previous]

    def column_sum(target, jj, owner, first, last, fresh):
        ends = [meta_s[1, g * 8 + owner * 4 + jj] for g in range(first, last)]
        for m in range(4):
            rows = pl.ds(m * BS, BS)
            total = products[m][ends[0]] if fresh else target[jj, rows]
            for end in ends[1 if fresh else 0 :]:
                total = total + products[m][end]
            target[jj, rows] = total

    def fold():
        for jj in range(4):
            column_sum(sib_send, jj, 1 - core, 0, FOLDED, True)
            column_sum(partial, jj, core, 0, FOLDED, True)

    def sib_copy(jj):
        return remote(SEND_SIB + jj, sib_send.at[jj], sib_recv.at[jj], sibling)


    def run(items, staged, c):
        for item in items:
            if item == 200:
                stage_source(staged, c)
                staged += 1
            elif item < 0:
                gather_copy(-1 - item).wait_recv()
            else:
                gather_copy(item).start()

    def sections(c):
        found, items, staged = [], [], 0
        for item in PROGRAMS[c] + (999,):
            if item == 999:
                found.append((items, staged))
                staged += items.count(200)
                items = []
            else:
                items.append(item)
        return found

    done = 0
    for n, (first, second) in enumerate(zip(sections(0), sections(1))):
        if first[0]:
            pl.when(core == 0)(functools.partial(run, *first, 0))
        if second[0]:
            pl.when(core == 1)(functools.partial(run, *second, 1))
        if n == len(SHARED):
            break
        if SHARED[n] == 300:
            multiply(done)
            done += STEP
        else:
            {400: sort_slots, 401: send_slots, 402: forward_slots, 500: fold}[SHARED[n]]()

    for jj in range(4):
        column_sum(sib_send, jj, 1 - core, FOLDED, NG, False)
        sib_copy(jj).start()
    for jj in range(4):
        column_sum(partial, jj, core, FOLDED, NG, False)

    half = BS // 2

    def exponent(value):
        largest = jnp.max(jnp.abs(value), axis=0, keepdims=True)
        return jnp.ceil(jnp.log2(jnp.maximum(largest, 1e-30)))

    def encode(value, power):
        scaled = jnp.round(value * jnp.exp2(15.0 - power))
        return jnp.clip(scaled, -32767.0, 32767.0).astype(I32).astype(jnp.int16)

    def decode(code, power):
        return code.astype(I32).astype(F32) * jnp.exp2(power - 15.0)

    def powers(first, second):
        rows = [jnp.broadcast_to(p.astype(I32), (8, BS)) for p in (first, second)]
        return jnp.concatenate(rows, axis=0).astype(jnp.int16)

    def read_powers(ref, side, jj):
        rows = ref[side, jj, pl.ds(half, 16)].astype(I32).astype(F32)
        return rows[0:1], rows[8:9]

    def drain(c, first, last):
        sent = [n for n, copy in enumerate(COPIES) if copy["ex"] == c]
        for n in sent[first:last]:
            gather_copy(n).wait_send()

    def drain_gather(first, last):
        pl.when(core == 0)(functools.partial(drain, 0, first, last))
        pl.when(core == 1)(functools.partial(drain, 1, first, last))

    def x_copy(jj, what):
        side, stage_of = what % 2, what // 2
        src = (half_send, near_send, full_send)[stage_of].at[side, jj]
        dst = (half_recv, near_recv, full_recv)[stage_of].at[side, jj]
        device = along_xy(1, 0) if side == 0 else along_xy(-1, 0)
        return remote(SEND_X + jj * 6 + what, src, dst, device)

    drain_gather(0, 16)
    near_powers = []
    for jj in range(4):
        sib_copy(jj).wait_recv()
        partial[jj] = partial[jj] + sib_recv[jj]
        for side in range(2):
            far = partial[jj, pl.ds(2 * BS + side * half, half)]
            near = partial[jj, pl.ds((BS + half) if side == 0 else 3 * BS, half)]
            far_power, near_power = exponent(far), exponent(near)
            half_send[side, jj, pl.ds(0, half)] = encode(far, far_power)
            half_send[side, jj, pl.ds(half, 16)] = powers(far_power, near_power)
            x_copy(jj, side).start()
            near_powers.append(near_power)
    for jj in range(4):
        for side in range(2):
            near = partial[jj, pl.ds((BS + half) if side == 0 else 3 * BS, half)]
            near_send[side, jj] = encode(near, near_powers[2 * jj + side])
            x_copy(jj, 2 + side).start()
    drain_gather(16, len(COPIES))
    for jj in range(4):
        for side in range(2):
            x_copy(jj, side).wait_recv()
            power, _ = read_powers(half_recv, side, jj)
            own = partial[jj, pl.ds(BS if side == 0 else 3 * BS + half, half)]
            value = own + decode(half_recv[side, jj, pl.ds(0, half)], power)
            power = exponent(value)
            full_send[side, jj, pl.ds(0, half)] = encode(value, power)
            full_send[side, jj, pl.ds(half, 16)] = powers(power, power)
            x_copy(jj, 4 + side).start()
    for n in range(N_SMALL):
        small_copy(n).wait_send()
    for jj in range(4):
        sib_copy(jj).wait_send()
        for what in range(4):
            x_copy(jj, what).wait_send()
    stores = []
    for jj in range(4):
        for what in (2, 3, 4, 5):
            x_copy(jj, what).wait_recv()
        total = []
        for part in range(2):
            value = partial[jj, pl.ds(part * half, half)]
            _, power = read_powers(half_recv, 1 - part, jj)
            value = value + decode(near_recv[1 - part, jj], power)
            power, _ = read_powers(full_recv, part, jj)
            total.append(value + decode(full_recv[part, jj, pl.ds(0, half)], power))
        total = jnp.concatenate(total, axis=0)
        square = total * total
        squared[jj] = square
        stores.append(pltpu.make_async_copy(squared.at[jj], squares.at[jj], local_sem.at[9 + jj]))
        stores[-1].start()
        sums_xy[0, jj : jj + 1, :] = jnp.sum(square, axis=0, keepdims=True)

    def xy_copy(n):
        dx, dy = xy_peers[n]
        slot = ((-dx) % NX) * NY + (-dy) % NY
        return remote(SEND_SUM, sums_xy.at[0], sums_xy.at[slot], along_xy(dx, dy))

    def z_copy(n):
        d = (4, 3, 5, 2, 6, 1, 7)[n]
        return remote(SEND_SUM + 1, sums_z.at[0], sums_z.at[(-d) % NZ], along_z(d))

    xy_all = sums_xy.at[pl.ds(1, 15)]
    z_all = sums_z.at[pl.ds(1, 7)]
    xy_round = remote(SEND_SUM, xy_all, xy_all, along_xy(1, 0))
    z_round = remote(SEND_SUM + 1, z_all, z_all, along_z(1))
    for n in range(15):
        xy_copy(n).start()
    total = sums_xy[0]
    for jj in range(4):
        x_copy(jj, 4).wait_send()
        x_copy(jj, 5).wait_send()
        stores[jj].wait()
    xy_round.wait_recv()
    for n in range(1, 16):
        total = total + sums_xy[n]
    sums_z[0] = total
    for n in range(7):
        z_copy(n).start()
    xy_round.wait_send()
    z_round.wait_recv()
    for n in range(1, NZ):
        total = total + sums_z[n]
    scale[...] = total / (NY * NZ * 4 * BS) + 1e-6
    last = pltpu.make_async_copy(scale, sums, local_sem.at[13])
    last.start()
    z_round.wait_send()
    last.wait()


def body(left_blocks, left_slots, right_blocks, right_slots, out_slots):
    any_spec = pl.BlockSpec(memory_space=pl.ANY)
    squares, sums = pl.pallas_call(
        kernel,
        out_shape=(
            jax.ShapeDtypeStruct((4, BS, BS), F32),
            jax.ShapeDtypeStruct((4, BS), F32),
        ),
        in_specs=[any_spec] * 5,
        out_specs=(any_spec, any_spec),
        scratch_shapes=[
            pltpu.VMEM((65, BS, BS), BF16),
            pltpu.VMEM((NY, NZ, 2, A_ROWS, BS), BF16),
            pltpu.VMEM((NZ, NY, 2, B_ROWS, BS), BF16),
            pltpu.VMEM((32 * 4, BS, BS), BF16),
            pltpu.VMEM((NONE + 1, BS, BS), F32),
            pltpu.VMEM((NONE + 1, BS, BS), F32),
            pltpu.VMEM((NONE + 1, BS, BS), F32),
            pltpu.VMEM((NONE + 1, BS, BS), F32),
            pltpu.VMEM((1, BS), I32),
            pltpu.VMEM((NY, NZ, 1, BS), I32),
            pltpu.VMEM((8, BS), I32),
            pltpu.SMEM((8, BS), I32),
            pltpu.SMEM((1, 64), I32),
            pltpu.SMEM((1, 4), I32),
            pltpu.SMEM((1, 32), I32),
            pltpu.VMEM((4, ROWS, BS), F32),
            pltpu.VMEM((4, ROWS, BS), F32),
            pltpu.VMEM((4, ROWS, BS), F32),
            pltpu.VMEM((2, 4, BS // 2 + 16, BS), jnp.int16),
            pltpu.VMEM((2, 4, BS // 2, BS), jnp.int16),
            pltpu.VMEM((2, 4, BS // 2 + 16, BS), jnp.int16),
            pltpu.VMEM((2, 4, BS // 2 + 16, BS), jnp.int16),
            pltpu.VMEM((2, 4, BS // 2, BS), jnp.int16),
            pltpu.VMEM((2, 4, BS // 2 + 16, BS), jnp.int16),
            pltpu.VMEM((16, 4, BS), F32),
            pltpu.VMEM((NZ, 4, BS), F32),
            pltpu.VMEM((4, BS), F32),
            pltpu.VMEM((4, BS, BS), F32),
            pltpu.SemaphoreType.DMA((N_SEM,)),
            pltpu.SemaphoreType.DMA((N_SEM,)),
            pltpu.SemaphoreType.DMA((14,)),
        ],
        compiler_params=pltpu.CompilerParams(
            collective_id=0, has_side_effects=True, vmem_limit_bytes=60 * 2**20
        ),
        name="expand_and_sum",
    )(
        left_slots,
        right_slots,
        out_slots,
        left_blocks.reshape(64, BS, BS),
        right_blocks.reshape(ROWS, BS),
    )
    return (squares / sums[:, None, :])[None]


def solution(mesh):
    return jax.shard_map(
        body,
        mesh=mesh,
        in_specs=(
            P(("row", "col"), "layer", None, None),
            P(("row", "col"), "layer"),
            P("layer", ("row", "col"), None, None),
            P("layer", ("row", "col")),
            P(("row", "col"), None),
        ),
        out_specs=P(("row", "col"), "layer", None, None),
        check_vma=False,
    )
```

```python
import functools

import jax
import jax.numpy as jnp
from jax import lax
from jax.experimental import pallas as pl
from jax.experimental.pallas import tpu as pltpu
from jax.sharding import PartitionSpec as P

MESH = pl.DeviceIdType.MESH
F32 = jnp.float32
BF16 = jnp.bfloat16
I32 = jnp.int32

BS = 128
NY, NZ, NX = 4, 8, 4
ROWS = 4 * BS
A_ROWS, B_ROWS = 304, 208
A_CUT, B_CUT = 160, 96
Z_INDEX = {0: 0, 1: 1, -1: 2, 2: 3, -2: 4, 3: 5, -3: 6, 4: 7}
Y_INDEX = {0: 0, 1: 1, -1: 2, 2: 3}
SOURCES = (
    (0, 0), (1, 2), (2, 2), (2, 1), (1, 0), (0, 1), (2, 0), (0, 2), (0, 3), (0, 4), (1, 1), (3, 1),
    (3, 0), (1, 3), (2, 4), (3, 2), (1, 4), (2, 3), (0, 6), (0, 5), (3, 3), (3, 4), (2, 5), (2, 6),
    (1, 6), (1, 5), (0, 7), (3, 6), (3, 5), (2, 7), (1, 7), (3, 7),
)
GROUPS = (4, 6, 8, 4, 4, 2, 2, 2)
PROGRAMS = (
    (
        8, 5, 0, 13, 54, 999, 48, 16, 20, -6, -7, 7, -14, -15, 15, 65, 999, 89, 60, -56, -8, -50,
        91, -55, -49, -16, 50, 56, 70, 75, -81, -66, -61, 61, 94, 200, 66, -23, -82, -85, 90, -51,
        -19, -57, 999, -86, 51, 200, 200, 200, 57, -76, -71, 97, 92, 200, 76, 200, 200, 200, 999,
        71, 200, 999, 200, 200, -87, 999, -29, 999, -26, -67, 67, 200, 200, -62, 62, 95, 200, 999,
        -83, -58, 200, 200, -52, 93, 200, 200, 200, 999, -32, -77, 77, 59, -72, 72, -35, 58, 98,
        200, 200, 53, 52, 200, 999, 999, -84, 999, 999, -68, 68, 69, -63, 96, 64, 63, -88, 999, -78,
        79, 200, 200, 78, 200, 200, -73, 73, 99, 74, -53, 999, 999, -41, -59, -89, 999, -69, -38,
        200, 200, 999, -44, -64, 200, 200, 200, -47, -74, -79, 999, 200, 999,
    ),
    (
        9, 999, 6, 1, 14, 200, 49, 55, 17, 21, -9, -10, 10, -1, -2, 2, 24, 27, -17, 80, -22, -21,
        84, 999, -11, 18, -18, -3, 30, 22, 3, 33, 11, -25, 81, 23, -28, 28, 19, 26, 85, -95, 29,
        200, 25, -92, 999, -12, -31, 200, -4, 31, -34, 34, 86, 36, 12, 200, -90, 39, 82, 999, -98,
        200, 200, 35, 32, 4, -93, 200, 200, 999, -27, -30, -24, 200, -91, 200, 999, 200, 999, -20,
        200, 200, 999, -96, 200, 200, 200, 200, 200, 999, -5, -13, 42, 45, 83, -94, 999, 999, 200,
        -37, -40, 40, 87, 999, 41, -33, -36, 38, -99, 200, 37, 200, 200, 999, 999, -60, -54, -43,
        43, 44, -46, 47, 46, -97, 88, 200, 200, 200, 200, 999, 999, 999, -39, -100, 200, -42, 200,
        999, -48, -45, -65, 200, -70, -75, -80, 200, 200, 999, 200, 999,
    ),
)
SHARED = (401, 402, 400) + (300,) * 13 + (500,) + (300,) * 3
STEP = 8
NG = len(GROUPS)
FOLDED = 5
NONE = 128


def wrap(value, count):
    value = value % count
    return value - count if value > count // 2 else value


def gather_copies():
    plans = {}

    def part(kind, sign, whole):
        size, cut = (A_ROWS, A_CUT) if kind == 0 else (B_ROWS, B_CUT)
        if whole:
            return 0, size
        return (0, cut) if sign == 1 else (cut, size - cut)

    def plan(key, kind, axis, sign, d, other, form):
        index, count = ((Y_INDEX, NY), (Z_INDEX, NZ))[axis]
        src = (index[-sign * (d - 1)], 1)
        dst = (index[wrap(-sign * d, count)], 1)
        first_axis = 0 if kind == 0 else 1
        order = (lambda v: (v, other)) if axis == first_axis else (lambda v: (other, v))
        plans[key] = dict(
            kind=kind, axis=axis, sign=sign, src=order(src), dst=order(dst),
            rows=part(kind, sign, d < count // 2), form=form,
        )

    for sign in (1, -1):
        for d in range(1, 5):
            plan(("Az", sign, d), 0, 1, sign, d, (0, 1), "own" if d == 1 else "pass")
        for d in (1, 2):
            plan(("By", sign, d), 1, 0, sign, d, (0, 1), "own" if d == 1 else "pass")
    a_waves = ((0, 1), (1, 2), (3, 2), (5, 2), (7, 1))
    b_waves = ((0, 1), (1, 2), (3, 1))
    for w, wave in enumerate(a_waves):
        for sign in (1, -1):
            for d in (1, 2):
                form = "last" if d == 2 else "pass" if w else "own"
                plan(("Ay", w, sign, d), 0, 0, sign, d, wave, form)
    for v, wave in enumerate(b_waves):
        for sign in (1, -1):
            for d in range(1, 5):
                form = "last" if d == 4 else "pass" if v or d > 1 else "own"
                plan(("Bz", v, sign, d), 1, 1, sign, d, wave, form)
    copies = []
    for p in plans.values():
        agent = 1 - p["kind"]
        if p["form"] == "own":
            copies += [dict(p, ex=c, rc=agent, lay=c) for c in (0, 1)]
        elif p["form"] == "last":
            copies += [dict(p, ex=agent, rc=c, lay=c) for c in (0, 1)]
        else:
            copies.append(dict(p, ex=agent, rc=agent, lay=2))

    def push(kind, where):
        agent = 1 - kind
        rows = (0, A_ROWS if kind == 0 else B_ROWS)
        copies.append(
            dict(kind=kind, src=where, dst=where, rows=rows, form="push", ex=agent, rc=1 - agent, lay=1 - agent)
        )

    for wave in a_waves[1:]:
        push(0, ((0, 1), wave))
    for wave in a_waves:
        push(0, ((1, 2), wave))
    push(1, ((0, 1), (1, 2)))
    push(1, ((0, 1), (3, 1)))
    for wave in b_waves:
        for first in (1, 3, 5):
            push(1, ((first, 2), wave))
    return copies


COPIES = gather_copies()
N_SMALL = 7 + 3
N_X = 4 * 6
N_SUM = 4
SEND_SMALL = len(COPIES)
SEND_SIB = SEND_SMALL + N_SMALL
SEND_X = SEND_SIB + 4
SEND_SUM = SEND_X + N_X
N_SEM = SEND_SUM + N_SUM


def to_column(row, eye):
    return jnp.sum(jnp.where(eye, jnp.broadcast_to(row, (BS, BS)), 0), axis=1, keepdims=True)


def kernel(
    left_slots, right_slots, out_slots, left, right, squares, sums,
    left_set, gather_a, gather_b, stage, products_0, products_1, products_2, products_3, slots_row, slots, meta, meta_s,
    left_s, right_s, out_s, sib_send, sib_recv, partial, half_send, near_send, full_send,
    half_recv, near_recv, full_recv,
    sums_xy, guests_xy, guest_sum, sums_z, scale, squared, send_sem, recv_sem, local_sem,
):
    y, z, layer = lax.axis_index("row"), lax.axis_index("col"), lax.axis_index("layer")
    x, core = layer >> 1, layer & 1
    products = (products_0, products_1, products_2, products_3)

    ys = [y] + [(y + d) & (NY - 1) for d in range(1, NY)]
    zs = [z] + [(z + d) & (NZ - 1) for d in range(1, NZ)]
    xs = [x] + [(x + d) & (NX - 1) for d in range(1, NX)]
    layers = [layer] + [xs[d] * 2 + core for d in range(1, NX)]

    def along_y(d):
        return (ys[d % NY], z, layer)

    def along_z(d):
        return (y, zs[d % NZ], layer)

    def along_xy(dx, dy):
        return (ys[dy % NY], z, layers[dx % NX])

    def at_core(device, c):
        return (device[0], device[1], x * 2 + c)

    sibling = (y, z, x * 2 + (1 - core))
    xy_peers = [(dx, dy) for dx in range(NX) for dy in range(NY) if dx or dy]
    xy_peers.sort(key=lambda p: -min(p[0], NX - p[0]) - min(p[1], NY - p[1]))

    barrier = pltpu.get_barrier_semaphore()
    peers = [along_z(d) for d in (4, 3, 5, 2, 6, 1, 7)] + [along_y(d) for d in (2, 1, 3)]
    peers += [along_xy(1, 0), along_xy(-1, 0), sibling]
    peers += [at_core(p, 1 - core) for p in (along_z(1), along_z(-1), along_y(1), along_y(-1))]
    for peer in peers:
        pl.semaphore_signal(barrier, 1, device_id=peer, device_id_type=MESH)
    local = [
        pltpu.make_async_copy(right_slots, right_s, local_sem.at[0]),
        pltpu.make_async_copy(left_slots, left_s, local_sem.at[1]),
        pltpu.make_async_copy(out_slots, out_s, local_sem.at[2]),
        pltpu.make_async_copy(left, left_set.at[pl.ds(0, 64)], local_sem.at[3]),
    ] + [
        pltpu.make_async_copy(right.at[pl.ds(q * BS, BS)], stage.at[q], local_sem.at[4 + q])
        for q in range(4)
    ]
    for copy in local:
        copy.start()
    left_set[64] = jnp.zeros((BS, BS), BF16)
    for m in range(4):
        products[m][NONE] = jnp.zeros((BS, BS), F32)
    pl.semaphore_wait(barrier, len(peers))

    def remote(number, src, dst, device):
        return pltpu.make_async_remote_copy(
            src_ref=src, dst_ref=dst, send_sem=send_sem.at[number], recv_sem=recv_sem.at[number],
            device_id=device, device_id_type=MESH,
        )

    def gather_copy(n):
        copy = COPIES[n]
        buffer = (gather_a, gather_b)[copy["kind"]]
        row, rows = copy["rows"]

        def place(where):
            index = [first if count == 1 else pl.ds(first, count) for first, count in where]
            lay = pl.ds(0, 2) if copy["lay"] == 2 else copy["lay"]
            return buffer.at[index[0], index[1], lay, pl.ds(row, rows)]

        if copy["form"] == "push":
            device = sibling
        else:
            along = along_z if copy["axis"] else along_y
            device = at_core(along(copy["sign"]), copy["rc"])
        if copy["form"] == "own":
            source = right.at[pl.ds((0 if copy["kind"] == 0 else A_ROWS) + row, rows)]
        else:
            source = place(copy["src"])
        return remote(n, source, place(copy["dst"]), device)

    def small_copy(n):
        if n < 7:
            d = n + 1
            return remote(
                SEND_SMALL + n, slots.at[0, 0], slots.at[0, Z_INDEX[wrap(-d, NZ)]], along_z(d)
            )
        d = n - 6
        return remote(SEND_SMALL + n, slots.at[0], slots.at[Y_INDEX[wrap(-d, NY)]], along_y(d))

    lane = lax.broadcasted_iota(I32, (1, BS), 1)

    def send_slots():
        local[0].wait()
        row = jnp.zeros((1, BS), I32)
        for q in range(4):
            row = jnp.where((lane & 3) == q, right_s[0, q], row)
        slots[0, 0] = row
        for n in range(7):
            small_copy(n).start()

    def forward_slots():
        for n in range(7):
            small_copy(n).wait_recv()
        for n in range(7, N_SMALL):
            small_copy(n).start()

    def sort_slots():
        for n in range(7, N_SMALL):
            small_copy(n).wait_recv()
        row_id = lax.broadcasted_iota(I32, (BS, BS), 0)
        lane_id = lax.broadcasted_iota(I32, (BS, BS), 1)
        eye = row_id == lane_id
        slot = jnp.zeros((1, BS), I32)
        for p, (yi, zi) in enumerate(SOURCES):
            slot = jnp.where((lane >> 2) == p, slots[yi, zi], slot)
        group = jnp.zeros((1, BS), I32)
        first = 0
        for size in GROUPS[:-1]:
            first += size
            group = group + ((lane >> 2) >= first).astype(I32)
        segment = group * 8 + (slot & 7)
        key = segment * BS + lane
        key_column = to_column(key, eye)
        rank = jnp.sum((key_column < key).astype(I32), axis=0, keepdims=True)
        segment_column = key_column >> 7
        before = jnp.sum((segment_column < segment).astype(I32), axis=0, keepdims=True)
        opens = (before == rank).astype(I32)
        packed = (rank << 16) | (opens << 15) | (slot << 7) | lane
        packed_column = to_column(packed, eye)
        here = (packed_column >> 16) == lane_id
        meta[0:1, :] = jnp.sum(jnp.where(here, packed_column & 0xFFFF, 0), axis=0, keepdims=True)
        upto = jnp.sum((segment_column <= lane_id).astype(I32), axis=0, keepdims=True)
        count = jnp.sum((segment_column == lane_id).astype(I32), axis=0, keepdims=True)
        meta[1:2, :] = jnp.where(count > 0, upto - 1, NONE)
        local[1].wait()
        inverse = [jnp.full((1, BS), 64, I32), jnp.full((1, BS), 64, I32)]
        for n in range(64):
            place = left_s[0, n]
            for h in range(2):
                inverse[h] = jnp.where(lane + h * BS == place, n, inverse[h])
        meta[2:3, :] = inverse[0]
        meta[3:4, :] = inverse[1]
        copy = pltpu.make_async_copy(meta, meta_s, local_sem.at[8])
        copy.start()
        copy.wait()
        for copy in local[2:]:
            copy.wait()

    def stage_source(p, c):
        if p == 0:
            return
        yi, zi = SOURCES[p]
        a_tail = A_ROWS - 2 * BS
        b_head = BS - a_tail
        stage[4 * p] = gather_a[yi, zi, c, pl.ds(0, BS)]
        stage[4 * p + 1] = gather_a[yi, zi, c, pl.ds(BS, BS)]
        stage[4 * p + 2, pl.ds(0, a_tail)] = gather_a[yi, zi, c, pl.ds(2 * BS, a_tail)]
        stage[4 * p + 2, pl.ds(a_tail, b_head)] = gather_b[zi, yi, c, pl.ds(0, b_head)]
        stage[4 * p + 3] = gather_b[zi, yi, c, pl.ds(b_head, BS)]

    def multiply(start):
        for t in range(start, start + STEP):
            word = meta_s[0, t]
            block, slot, opens = word & 127, (word >> 7) & 255, word >> 15
            k, j = slot >> 3, slot & 7
            chosen = []
            for m in range(4):
                r = out_s[0, xs[m] * 8 + j] >> 3
                at = r * 32 + k
                chosen.append(left_set[meta_s[2 + (at >> 7), at & 127]])
            product = jnp.dot(
                jnp.concatenate(chosen, axis=0), stage[block], preferred_element_type=F32
            )
            previous = opens * NONE + (1 - opens) * (t - 1)
            for m in range(4):
                rows = product[m * BS : (m + 1) * BS]
                products[m][t] = rows + products[m][previous]

    def column_sum(target, jj, owner, first, last, fresh):
        ends = [meta_s[1, g * 8 + owner * 4 + jj] for g in range(first, last)]
        for m in range(4):
            rows = pl.ds(m * BS, BS)
            total = products[m][ends[0]] if fresh else target[jj, rows]
            for end in ends[1 if fresh else 0 :]:
                total = total + products[m][end]
            target[jj, rows] = total

    def fold():
        for jj in range(4):
            column_sum(sib_send, jj, 1 - core, 0, FOLDED, True)
            column_sum(partial, jj, core, 0, FOLDED, True)

    def sib_copy(jj):
        return remote(SEND_SIB + jj, sib_send.at[jj], sib_recv.at[jj], sibling)


    def run(items, staged, c):
        for item in items:
            if item == 200:
                stage_source(staged, c)
                staged += 1
            elif item < 0:
                gather_copy(-1 - item).wait_recv()
            else:
                gather_copy(item).start()

    def sections(c):
        found, items, staged = [], [], 0
        for item in PROGRAMS[c] + (999,):
            if item == 999:
                found.append((items, staged))
                staged += items.count(200)
                items = []
            else:
                items.append(item)
        return found

    done = 0
    for n, (first, second) in enumerate(zip(sections(0), sections(1))):
        if first[0]:
            pl.when(core == 0)(functools.partial(run, *first, 0))
        if second[0]:
            pl.when(core == 1)(functools.partial(run, *second, 1))
        if n == len(SHARED):
            break
        if SHARED[n] == 300:
            multiply(done)
            done += STEP
        else:
            {400: sort_slots, 401: send_slots, 402: forward_slots, 500: fold}[SHARED[n]]()

    for jj in range(4):
        column_sum(sib_send, jj, 1 - core, FOLDED, NG, False)
        sib_copy(jj).start()
    for jj in range(4):
        column_sum(partial, jj, core, FOLDED, NG, False)

    half = BS // 2

    def exponent(value):
        largest = jnp.max(jnp.abs(value), axis=0, keepdims=True)
        return jnp.ceil(jnp.log2(jnp.maximum(largest, 1e-30)))

    def encode(value, power):
        scaled = jnp.round(value * jnp.exp2(15.0 - power))
        return jnp.clip(scaled, -32767.0, 32767.0).astype(I32).astype(jnp.int16)

    def decode(code, power):
        return code.astype(I32).astype(F32) * jnp.exp2(power - 15.0)

    def powers(first, second):
        rows = [jnp.broadcast_to(p.astype(I32), (8, BS)) for p in (first, second)]
        return jnp.concatenate(rows, axis=0).astype(jnp.int16)

    def read_powers(ref, side, jj):
        rows = ref[side, jj, pl.ds(half, 16)].astype(I32).astype(F32)
        return rows[0:1], rows[8:9]

    def drain(c, first, last):
        sent = [n for n, copy in enumerate(COPIES) if copy["ex"] == c]
        for n in sent[first:last]:
            gather_copy(n).wait_send()

    def drain_gather(first, last):
        pl.when(core == 0)(functools.partial(drain, 0, first, last))
        pl.when(core == 1)(functools.partial(drain, 1, first, last))

    def x_copy(jj, what):
        side, stage_of = what % 2, what // 2
        src = (half_send, near_send, full_send)[stage_of].at[side, jj]
        dst = (half_recv, near_recv, full_recv)[stage_of].at[side, jj]
        device = along_xy(1, 0) if side == 0 else along_xy(-1, 0)
        return remote(SEND_X + jj * 6 + what, src, dst, device)

    drain_gather(0, 16)
    near_powers = []
    for jj in range(4):
        sib_copy(jj).wait_recv()
        partial[jj] = partial[jj] + sib_recv[jj]
        for side in range(2):
            far = partial[jj, pl.ds(2 * BS + side * half, half)]
            near = partial[jj, pl.ds((BS + half) if side == 0 else 3 * BS, half)]
            far_power, near_power = exponent(far), exponent(near)
            half_send[side, jj, pl.ds(0, half)] = encode(far, far_power)
            half_send[side, jj, pl.ds(half, 16)] = powers(far_power, near_power)
            x_copy(jj, side).start()
            near_powers.append(near_power)
    for jj in range(4):
        for side in range(2):
            near = partial[jj, pl.ds((BS + half) if side == 0 else 3 * BS, half)]
            near_send[side, jj] = encode(near, near_powers[2 * jj + side])
            x_copy(jj, 2 + side).start()
    drain_gather(16, len(COPIES))
    for jj in range(4):
        for side in range(2):
            x_copy(jj, side).wait_recv()
            power, _ = read_powers(half_recv, side, jj)
            own = partial[jj, pl.ds(BS if side == 0 else 3 * BS + half, half)]
            value = own + decode(half_recv[side, jj, pl.ds(0, half)], power)
            power = exponent(value)
            full_send[side, jj, pl.ds(0, half)] = encode(value, power)
            full_send[side, jj, pl.ds(half, 16)] = powers(power, power)
            x_copy(jj, 4 + side).start()
    for n in range(N_SMALL):
        small_copy(n).wait_send()
    for jj in range(4):
        sib_copy(jj).wait_send()
        for what in range(4):
            x_copy(jj, what).wait_send()
    stores = []
    for jj in range(4):
        for what in (2, 3, 4, 5):
            x_copy(jj, what).wait_recv()
        total = []
        for part in range(2):
            value = partial[jj, pl.ds(part * half, half)]
            _, power = read_powers(half_recv, 1 - part, jj)
            value = value + decode(near_recv[1 - part, jj], power)
            power, _ = read_powers(full_recv, part, jj)
            total.append(value + decode(full_recv[part, jj, pl.ds(0, half)], power))
        total = jnp.concatenate(total, axis=0)
        square = total * total
        squared[jj] = square
        stores.append(pltpu.make_async_copy(squared.at[jj], squares.at[jj], local_sem.at[9 + jj]))
        stores[-1].start()
        sums_xy[0, jj : jj + 1, :] = jnp.sum(square, axis=0, keepdims=True)

    def xy_copy(n):
        dx, dy = xy_peers[n]
        slot = ((-dx) % NX) * NY + (-dy) % NY
        return remote(SEND_SUM, sums_xy.at[0], sums_xy.at[slot], along_xy(dx, dy))

    def z_copy(n):
        d = (4, 3, 5, 2, 6, 1, 7)[n]
        return remote(SEND_SUM + 1, sums_z.at[0], sums_z.at[(-d) % NZ], along_z(d))

    def guest_xy_copy(n):
        dx, dy = ([(0, 0)] + xy_peers)[n]
        slot = ((-dx) % NX) * NY + (-dy) % NY
        target = (ys[dy % NY], z, layers[dx % NX] + 1)
        return remote(SEND_SUM + 2, sums_xy.at[0], guests_xy.at[slot], target)

    def guest_z_copy(n):
        d = (4, 3, 5, 2, 6, 1, 7, 0)[n]
        target = (y, zs[d], layer - 1)
        return remote(SEND_SUM + 3, guest_sum, sums_z.at[(-d) % NZ], target)

    def drain_x():
        for jj in range(4):
            x_copy(jj, 4).wait_send()
            x_copy(jj, 5).wait_send()
            stores[jj].wait()

    guest_xy_round = remote(SEND_SUM + 2, guests_xy, guests_xy, sibling)
    guest_z_round = remote(SEND_SUM + 3, sums_z, sums_z, sibling)
    xy_all = sums_xy.at[pl.ds(1, 15)]
    z_all = sums_z.at[pl.ds(1, 7)]
    xy_round = remote(SEND_SUM, xy_all, xy_all, along_xy(1, 0))
    z_round = remote(SEND_SUM + 1, z_all, z_all, along_z(1))

    @pl.when(core == 0)
    def _():
        for n in (*range(1, 16), 0):
            guest_xy_copy(n).start()
        drain_x()
        guest_xy_round.wait_send()
        guest_z_round.wait_recv()

    @pl.when(core == 1)
    def _():
        for n in range(15):
            xy_copy(n).start()
        drain_x()
        xy_round.wait_recv()
        total = sums_xy[0]
        for n in range(1, 16):
            total = total + sums_xy[n]
        sums_z[0] = total
        for n in range(7):
            z_copy(n).start()
        guest_xy_round.wait_recv()
        total = guests_xy[0]
        for n in range(1, 16):
            total = total + guests_xy[n]
        guest_sum[...] = total
        for n in range(8):
            guest_z_copy(n).start()
        xy_round.wait_send()
        z_round.wait_recv()

    total = sums_z[0]
    for n in range(1, NZ):
        total = total + sums_z[n]
    scale[...] = total / (NY * NZ * 4 * BS) + 1e-6
    last = pltpu.make_async_copy(scale, sums, local_sem.at[13])
    last.start()

    @pl.when(core == 1)
    def _():
        z_round.wait_send()
        guest_z_round.wait_send()

    last.wait()


def body(left_blocks, left_slots, right_blocks, right_slots, out_slots):
    any_spec = pl.BlockSpec(memory_space=pl.ANY)
    squares, sums = pl.pallas_call(
        kernel,
        out_shape=(
            jax.ShapeDtypeStruct((4, BS, BS), F32),
            jax.ShapeDtypeStruct((4, BS), F32),
        ),
        in_specs=[any_spec] * 5,
        out_specs=(any_spec, any_spec),
        scratch_shapes=[
            pltpu.VMEM((65, BS, BS), BF16),
            pltpu.VMEM((NY, NZ, 2, A_ROWS, BS), BF16),
            pltpu.VMEM((NZ, NY, 2, B_ROWS, BS), BF16),
            pltpu.VMEM((32 * 4, BS, BS), BF16),
            pltpu.VMEM((NONE + 1, BS, BS), F32),
            pltpu.VMEM((NONE + 1, BS, BS), F32),
            pltpu.VMEM((NONE + 1, BS, BS), F32),
            pltpu.VMEM((NONE + 1, BS, BS), F32),
            pltpu.VMEM((1, BS), I32),
            pltpu.VMEM((NY, NZ, 1, BS), I32),
            pltpu.VMEM((8, BS), I32),
            pltpu.SMEM((8, BS), I32),
            pltpu.SMEM((1, 64), I32),
            pltpu.SMEM((1, 4), I32),
            pltpu.SMEM((1, 32), I32),
            pltpu.VMEM((4, ROWS, BS), F32),
            pltpu.VMEM((4, ROWS, BS), F32),
            pltpu.VMEM((4, ROWS, BS), F32),
            pltpu.VMEM((2, 4, BS // 2 + 16, BS), jnp.int16),
            pltpu.VMEM((2, 4, BS // 2, BS), jnp.int16),
            pltpu.VMEM((2, 4, BS // 2 + 16, BS), jnp.int16),
            pltpu.VMEM((2, 4, BS // 2 + 16, BS), jnp.int16),
            pltpu.VMEM((2, 4, BS // 2, BS), jnp.int16),
            pltpu.VMEM((2, 4, BS // 2 + 16, BS), jnp.int16),
            pltpu.VMEM((16, 4, BS), F32),
            pltpu.VMEM((16, 4, BS), F32),
            pltpu.VMEM((4, BS), F32),
            pltpu.VMEM((NZ, 4, BS), F32),
            pltpu.VMEM((4, BS), F32),
            pltpu.VMEM((4, BS, BS), F32),
            pltpu.SemaphoreType.DMA((N_SEM,)),
            pltpu.SemaphoreType.DMA((N_SEM,)),
            pltpu.SemaphoreType.DMA((14,)),
        ],
        compiler_params=pltpu.CompilerParams(
            collective_id=0, has_side_effects=True, vmem_limit_bytes=60 * 2**20
        ),
        name="expand_and_sum",
    )(
        left_slots,
        right_slots,
        out_slots,
        left_blocks.reshape(64, BS, BS),
        right_blocks.reshape(ROWS, BS),
    )
    return (squares / sums[:, None, :])[None]


def solution(mesh):
    return jax.shard_map(
        body,
        mesh=mesh,
        in_specs=(
            P(("row", "col"), "layer", None, None),
            P(("row", "col"), "layer"),
            P("layer", ("row", "col"), None, None),
            P("layer", ("row", "col")),
            P(("row", "col"), None),
        ),
        out_specs=P(("row", "col"), "layer", None, None),
        check_vma=False,
    )
```
